32 devices in a mesh: dp: 16 (over z, y, core), tensor: 2 (over x).
Axes of the slice: x: 2, y: 2, z: 4, core: 2. Of those that a mesh axis runs over, the one named last changes fastest.
Arguments:
- tokens: bfloat16 [16384, 1536], P(('dp', 'tensor')), may hold values from -6 to 6
- cotangent: bfloat16 [16384, 1536], P(('dp', 'tensor')), may hold values from -6 to 6
- lengths: int32 [64], replicated, may hold values from 1 to 1021, as said below
- sequence_adapter: int32 [64], replicated, may hold values from 0 to 7
- perm: int32 [16384], P(('dp', 'tensor')), may hold values from 0 to 16383, as said below
- dealt_position: int32 [16384], P(('dp', 'tensor')), may hold values from 0 to 16383, as said below
- block_norm_gain: float32 [1536], replicated, may hold values from 0.5 to 1.5
- gate_input_weight: bfloat16 [1536, 2, 3072], P('dp', None, 'tensor'), may hold values from -0.15625 to 0.15625
- rest_weight: bfloat16 [1536, 304], P('dp'), may hold values from -0.15625 to 0.15625
- filter_taps_input: float32 [5, 3072], P(None, 'tensor'), may hold values from -0.5 to 0.5
- filter_taps_bc: float32 [5, 256], replicated, may hold values from -0.5 to 0.5
- step_bias: float32 [48], P('tensor'), may hold values from -6.9 to -2.3
- head_decay_rate: float32 [48], P('tensor'), may hold values from 1 to 16
- skip_weight: float32 [48], P('tensor'), may hold values from 0.5 to 2
- gated_norm_gain: float32 [3072], P('tensor'), may hold values from 0.5 to 1.5
- output_weight: bfloat16 [3072, 1536], P('tensor', 'dp'), may hold values from -0.109375 to 0.109375
- adapter_down_in: bfloat16 [1536, 128], replicated, may hold values from -0.15625 to 0.15625
- adapter_up_gate_input: bfloat16 [128, 2, 3072], P(None, None, 'tensor'), may hold values from -1.5 to 1.5
- adapter_up_rest: bfloat16 [128, 304], replicated, may hold values from -1.5 to 1.5
- adapter_down_out: bfloat16 [3072, 128], P('tensor'), may hold values from -0.109375 to 0.109375
- adapter_up_out: bfloat16 [128, 1536], replicated, may hold values from -1.5 to 1.5
Outputs:
- output: bfloat16 [16384, 1536], P(('dp', 'tensor'))
- input_grad: bfloat16 [16384, 1536], P(('dp', 'tensor'))
- gradient_down_in: float32 [1536, 128], replicated
- gradient_up_gate_input: float32 [128, 2, 3072], P(None, None, 'tensor')
- gradient_up_rest: float32 [128, 304], replicated
- gradient_down_out: float32 [3072, 128], P('tensor')
- gradient_up_out: float32 [128, 1536], replicated
The draws below stay inside these ranges and needn't reach their ends.
Inputs may be any that keep to these rules, and one draw needn't show every extreme that they name: `lengths`: each run of 4 entries (the sequences of one dp index, end to end in the dealt order) sums to 1024; in each run one sequence is longer than 512 and the others together are shorter than 512. `perm`: A permutation; every device of the given order sends exactly 32 of its rows to each dp index, all to devices of its own tensor index. `dealt_position`: the inverse of perm.
All inputs are finite; a program needn't handle non-finite values.
Results may differ from the reference program's by a relative error of at most 0.012.
Values may be sent and summed in bfloat16 or wider, within the bound.
No kernel may reach another device: no remote copies, remote signals or barrier semaphores. Data moves between devices by JAX's collectives and lax.ppermute only.
A program may use at most 256 MiB of HBM per device.

```python
import math
from functools import partial
import jax
import jax.numpy as jnp
from jax import lax

MODEL_WIDTH = 1536
HEADS = 48
HEADDIM = 64
STATE = 128
SPAN = 256
ADAPTER_COUNT = 8
ADAPTER_RANK = 16
SEQ_GROUP = 4
GROUP = 1024
INNER_WIDTH = 3072
REST_COLUMNS = 304
ADAPTER_COLUMNS = 128
TOK_DEV = 512
TOKENS = 16384
SEQS = 64
N_DP = 16
N_TENSOR = 2


def deal_tables(key):
    key = jax.random.fold_in(key, 5)
    first_key, second_key = jax.random.split(key)
    device_count = N_DP * N_TENSOR
    per_peer = TOK_DEV // N_DP

    def shuffle(sub_key):
        return jax.random.permutation(sub_key, TOK_DEV)
    rows_to = jax.vmap(shuffle)(jax.random.split(first_key, device_count)).reshape(N_DP, N_TENSOR, TOK_DEV)
    rows_from = jax.vmap(shuffle)(jax.random.split(second_key, device_count)).reshape(N_DP, N_TENSOR, TOK_DEV)
    source = rows_to // per_peer
    within = rows_to % per_peer
    group_index = jnp.arange(N_DP, dtype=jnp.int32)[:, None, None]
    tensor_index = jnp.arange(N_TENSOR, dtype=jnp.int32)[None, :, None]
    slot = group_index * per_peer + within
    tensor_full = jnp.broadcast_to(tensor_index, source.shape)
    local_row = rows_from[source, tensor_full, slot]
    forward_map = ((source * N_TENSOR + tensor_index) * TOK_DEV + local_row).reshape(-1).astype(jnp.int32)
    backward_map = jnp.zeros_like(forward_map).at[forward_map].set(jnp.arange(forward_map.shape[0], dtype=jnp.int32))
    return (forward_map, backward_map)


def draw_perm(key, part):
    return deal_tables(key)[0]


def draw_dealt_position(key, part):
    return deal_tables(key)[1]


def draw_lengths(key, part):
    key = jax.random.fold_in(key, 11)
    short_key, place_key, chosen_key = jax.random.split(key, 3)
    shorts = jax.random.randint(short_key, (N_DP, SEQ_GROUP - 1), 1, TOK_DEV // 4 + 1)
    chosen = jax.random.randint(chosen_key, (), 0, N_DP)
    shorts = jnp.where(jnp.arange(N_DP)[:, None] == chosen, 1, shorts)
    longest = GROUP - jnp.sum(shorts, axis=1)
    place = jax.random.randint(place_key, (N_DP,), 0, SEQ_GROUP)
    slots = jnp.arange(SEQ_GROUP)[None, :]
    source_slot = jnp.clip(jnp.where(slots < place[:, None], slots, slots - 1), 0, SEQ_GROUP - 2)
    picked = jnp.take_along_axis(shorts, source_slot, axis=1)
    block_result = jnp.where(slots == place[:, None], longest[:, None], picked)
    return block_result.reshape(-1).astype(jnp.int32)


def plant(drawn, stream_key, low, high):
    index_at = [jax.random.randint(jax.random.fold_in(stream_key, axis), (), 0, length) for axis, length in enumerate(drawn.shape)]
    widest = drawn.shape.index(max(drawn.shape))
    beside = index_at[:widest] + [(index_at[widest] + 1) % drawn.shape[widest]] + index_at[widest + 1:]
    return drawn.at[tuple(index_at)].set(low).at[tuple(beside)].set(high)


def shard_levels(rng, shape, cuts, low, top_value):
    factor_of = 1.0
    for dim, blocks in cuts:
        draws = jax.random.uniform(jax.random.fold_in(jax.random.fold_in(rng, 6), dim), (blocks,), jnp.float32, low / len(cuts), top_value / len(cuts))
        factor_of = factor_of * jnp.repeat(jnp.exp(draws), shape[dim] // blocks).reshape((-1,) + (1,) * (len(shape) - 1 - dim))
    return factor_of


def centred(key, dims, spread, most, cuts=(), held_as=jnp.bfloat16):
    values = spread * jax.random.normal(key, dims, jnp.float32)
    if cuts:
        values = values * shard_levels(key, dims, cuts, -0.22, 0.18)
    return jnp.clip(values, -most, most).astype(held_as)


def setup_inputs(seed: int = 0) -> dict:
    splits = jax.random.split(jax.random.key(seed), 22)
    tokens = centred(splits[0], (TOKENS, MODEL_WIDTH), 1.0, 6.0, ((0, 32),))
    cotangent = centred(splits[1], (TOKENS, MODEL_WIDTH), 1.0, 6.0, ((0, 32),))
    lengths = draw_lengths(jax.random.fold_in(splits[21], 71), 0)
    sequence_adapter = plant(jax.random.randint(splits[3], (SEQS,), 0, ADAPTER_COUNT), jax.random.fold_in(splits[3], 1), 0, ADAPTER_COUNT - 1).astype(jnp.int32)
    perm = draw_perm(jax.random.fold_in(splits[21], 71), 0)
    dealt_position = draw_dealt_position(jax.random.fold_in(splits[21], 71), 0)
    block_norm_gain = jnp.clip(1.0 + 0.1 * jax.random.normal(splits[6], (MODEL_WIDTH,), jnp.float32), 0.5, 1.5)
    gate_input_weight = centred(splits[7], (MODEL_WIDTH, 2, INNER_WIDTH), MODEL_WIDTH ** -0.5, 0.15625, ((0, 16), (2, 2)))
    rest_weight = centred(splits[8], (MODEL_WIDTH, REST_COLUMNS), MODEL_WIDTH ** -0.5, 0.15625, ((0, 16),))
    filter_taps_input = jnp.clip(jax.random.uniform(splits[9], (5, INNER_WIDTH), jnp.float32, -0.5, 0.5) * shard_levels(splits[9], (5, INNER_WIDTH), ((1, 2),), -0.4, 0.0), -0.5, 0.5)
    filter_taps_bc = jnp.clip(jax.random.uniform(splits[10], (5, 2 * STATE), jnp.float32, -0.5, 0.5), -0.5, 0.5)
    step_bias = jnp.clip(-6.9 + 4.6000001430511475 * jax.random.uniform(splits[11], (HEADS,), jnp.float32) ** shard_levels(splits[11], (HEADS,), ((0, 2),), -0.2, 0.2), -6.9, -2.3)
    head_decay_rate = jnp.clip(jnp.exp(math.log(16.0) - 2.7725887 * jax.random.uniform(splits[12], (HEADS,), jnp.float32) ** shard_levels(splits[12], (HEADS,), ((0, 2),), -0.2, 0.2)), 1.0, 16.0)
    skip_weight = jnp.clip(0.5 + 1.5 * jax.random.uniform(splits[13], (HEADS,), jnp.float32) ** shard_levels(splits[13], (HEADS,), ((0, 2),), -0.2, 0.2), 0.5, 2.0)
    gated_norm_gain = jnp.clip(1.0 + 0.1 * jax.random.normal(splits[14], (INNER_WIDTH,), jnp.float32), 0.5, 1.5)
    output_weight = centred(splits[15], (INNER_WIDTH, MODEL_WIDTH), INNER_WIDTH ** -0.5, 0.109375, ((0, 2), (1, 16)))
    adapter_down_in = centred(splits[16], (MODEL_WIDTH, ADAPTER_COLUMNS), MODEL_WIDTH ** -0.5, 0.15625)
    adapter_up_gate_input = centred(splits[17], (ADAPTER_COLUMNS, 2, INNER_WIDTH), ADAPTER_RANK ** -0.5, 1.5, ((2, 2),))
    adapter_up_rest = centred(splits[18], (ADAPTER_COLUMNS, REST_COLUMNS), ADAPTER_RANK ** -0.5, 1.5)
    adapter_down_out = centred(splits[19], (INNER_WIDTH, ADAPTER_COLUMNS), INNER_WIDTH ** -0.5, 0.109375, ((0, 2),))
    adapter_up_out = centred(splits[20], (ADAPTER_COLUMNS, MODEL_WIDTH), ADAPTER_RANK ** -0.5, 1.5)
    return {"tokens": tokens, "cotangent": cotangent, "lengths": lengths, "sequence_adapter": sequence_adapter, "perm": perm, "dealt_position": dealt_position, "block_norm_gain": block_norm_gain, "gate_input_weight": gate_input_weight, "rest_weight": rest_weight, "filter_taps_input": filter_taps_input, "filter_taps_bc": filter_taps_bc, "step_bias": step_bias, "head_decay_rate": head_decay_rate, "skip_weight": skip_weight, "gated_norm_gain": gated_norm_gain, "output_weight": output_weight, "adapter_down_in": adapter_down_in, "adapter_up_gate_input": adapter_up_gate_input, "adapter_up_rest": adapter_up_rest, "adapter_down_out": adapter_down_out, "adapter_up_out": adapter_up_out}


epsilon = 1e-05

@jax.custom_vjp
def lowrank_rows(v):
    return lax.optimization_barrier(v.astype(jnp.bfloat16)).astype(jnp.float32)

@jax.custom_vjp
def lowrank_gradient(v):
    return v

def low_keep(v):
    return (lowrank_rows(v), None)

def low_pass(kept, grad):
    return (grad,)

def back_keep(v):
    return (v, None)

def back_low(kept, grad):
    return (lowrank_rows(grad),)
lowrank_rows.defvjp(low_keep, low_pass)
lowrank_gradient.defvjp(back_keep, back_low)

def shift_down(values, offset):
    padding = jnp.zeros((offset,) + values.shape[1:], values.dtype)
    return jnp.concatenate([padding, values[:-offset]], axis=0)

def conv_valid(segment):
    same_seq = []
    for offset in (1, 2, 3):
        before = jnp.concatenate([jnp.full((offset,), -1, jnp.int32), segment[:-offset]])
        same_seq.append((before == segment).astype(jnp.float32)[:, None])
    return same_seq

def causal_conv(values, kernel, same_seq):
    summed = kernel[3] * values + kernel[4]
    for offset in (1, 2, 3):
        summed = summed + kernel[3 - offset] * shift_down(values, offset) * same_seq[offset - 1]
    return jax.nn.silu(summed)

def ssd_block(carried_in, pieces, head_decay_rate, skip_weight):
    carry_state, seg_prev = carried_in
    inputs, b_block, c_block, step_sizes, segment = pieces
    highest_precision = lax.Precision.HIGHEST
    block_len = segment.shape[0]
    log_decay = -head_decay_rate[None, :] * step_sizes
    cumul = jnp.cumsum(log_decay, axis=0)
    span_total = cumul[-1]
    heads_first = cumul.T
    gaps = heads_first[:, :, None] - heads_first[:, None, :]
    causal = jnp.arange(block_len)[:, None] >= jnp.arange(block_len)[None, :]
    allowed = (causal & (segment[:, None] == segment[None, :])).astype(jnp.float32)
    decays = jnp.exp(jnp.minimum(gaps, 0.0)) * allowed[None, :, :]
    scores = jnp.dot(c_block, b_block.T, precision=highest_precision)
    weights = scores[None, :, :] * decays * step_sizes.T[:, None, :]
    outputs = jnp.einsum('hts,shp->thp', weights, inputs, precision=highest_precision)
    carried = (segment == seg_prev).astype(jnp.float32)
    from_state = jnp.einsum('tn,hpn->thp', c_block, carry_state, precision=highest_precision)
    outputs = outputs + (jnp.exp(cumul) * carried[:, None])[:, :, None] * from_state
    seg_end = segment[-1].astype(jnp.int32)
    kept_state = (seg_end == seg_prev).astype(jnp.float32)
    in_last = (segment == seg_end).astype(jnp.float32)
    coefficient = jnp.exp(span_total[None, :] - cumul) * step_sizes * in_last[:, None]
    carry_state = kept_state * jnp.exp(span_total)[:, None, None] * carry_state + jnp.einsum('sh,shp,sn->hpn', coefficient, inputs, b_block, precision=highest_precision)
    outputs = outputs + skip_weight[None, :, None] * inputs
    return ((carry_state, seg_end), outputs)

def ssd(inputs, b_matrix, c_matrix, step_sizes, segment, head_decay_rate, skip_weight):
    row_count, head_count, head_width = inputs.shape
    span_count = row_count // SPAN
    pieces = (inputs.reshape(span_count, SPAN, head_count, head_width), b_matrix.reshape(span_count, SPAN, b_matrix.shape[1]), c_matrix.reshape(span_count, SPAN, c_matrix.shape[1]), step_sizes.reshape(span_count, SPAN, head_count), segment.astype(jnp.int32).reshape(span_count, SPAN))
    start_state = jnp.zeros((head_count, head_width, b_matrix.shape[1]), jnp.float32)
    stepper = jax.checkpoint(partial(ssd_block, head_decay_rate=head_decay_rate, skip_weight=skip_weight))
    final_carry, outputs = lax.scan(stepper, (start_state, jnp.int32(-1)), pieces)
    return outputs.reshape(row_count, head_count, head_width)

def group_forward(residual_input, segment, adapter_select_mask, adapter_params, frozen):
    adapter_down_in, adapter_up_gate_input, adapter_up_rest, adapter_down_out, adapter_up_out = adapter_params
    block_norm_gain, gate_input_weight, rest_weight, filter_taps_input, filter_taps_bc, step_bias, head_decay_rate, skip_weight, gated_norm_gain, output_weight = frozen
    highest_precision = lax.Precision.HIGHEST
    row_count = residual_input.shape[0]
    inner_width = INNER_WIDTH
    state_dim = STATE
    heads_group = HEADS // N_TENSOR
    inner_width_group = heads_group * HEADDIM
    adapter_width = adapter_down_in.shape[1]
    normalized_input = lowrank_rows(residual_input * lax.rsqrt(lax.optimization_barrier(jnp.mean(residual_input * residual_input, axis=1, keepdims=True)) + epsilon) * block_norm_gain)
    middle_input = lowrank_rows(jnp.dot(normalized_input, adapter_down_in, precision=highest_precision) * adapter_select_mask)
    base_zx = jnp.dot(normalized_input, gate_input_weight, precision=highest_precision).reshape(row_count, 2, inner_width)
    plain_rest_output = jnp.dot(normalized_input, rest_weight, precision=highest_precision)
    same_seq = conv_valid(segment)
    gates = []
    scans = []
    for group in range(N_TENSOR):
        lower_column = group * inner_width_group
        middle_group = lowrank_gradient(middle_input)
        up_gate_input_group = adapter_up_gate_input[:, :, lower_column:lower_column + inner_width_group].reshape(adapter_width, 2 * inner_width_group)
        zx_group = lowrank_gradient(base_zx[:, :, lower_column:lower_column + inner_width_group] + jnp.dot(middle_group, up_gate_input_group, precision=highest_precision).reshape(row_count, 2, inner_width_group))
        rest_columns_group = lowrank_gradient(plain_rest_output + jnp.dot(middle_group, adapter_up_rest, precision=highest_precision))
        gates.append(zx_group[:, 0, :])
        x_group = lowrank_rows(causal_conv(zx_group[:, 1, :], filter_taps_input[:, lower_column:lower_column + inner_width_group], same_seq))
        bc_group = causal_conv(rest_columns_group[:, :2 * state_dim], filter_taps_bc, same_seq)
        b_group = lowrank_rows(bc_group[:, :state_dim])
        c_group = lowrank_rows(bc_group[:, state_dim:])
        head_lo = group * heads_group
        dt_lo = 2 * state_dim + head_lo
        steps_group = jax.nn.softplus(rest_columns_group[:, dt_lo:dt_lo + heads_group] + step_bias[head_lo:head_lo + heads_group])
        scanned = ssd(x_group.reshape(row_count, heads_group, HEADDIM), b_group, c_group, steps_group, segment, head_decay_rate[head_lo:head_lo + heads_group], skip_weight[head_lo:head_lo + heads_group])
        scans.append(lowrank_gradient(scanned.reshape(row_count, inner_width_group)))
    gate_pre = jnp.concatenate(gates, axis=1)
    scan_out = jnp.concatenate(scans, axis=1)
    gated = scan_out * jax.nn.silu(gate_pre)
    normalized_output = lowrank_rows(gated * lax.rsqrt(lax.optimization_barrier(jnp.mean(gated * gated, axis=1, keepdims=True)) + epsilon) * gated_norm_gain)
    middle_output = lowrank_rows(lowrank_gradient(jnp.dot(normalized_output, adapter_down_out, precision=highest_precision)) * adapter_select_mask)
    return residual_input + jnp.dot(normalized_output, output_weight, precision=highest_precision) + jnp.dot(middle_output, adapter_up_out, precision=highest_precision)

def reference(tokens, cotangent, lengths, sequence_adapter, perm, dealt_position, block_norm_gain, gate_input_weight, rest_weight, filter_taps_input, filter_taps_bc, step_bias, head_decay_rate, skip_weight, gated_norm_gain, output_weight, adapter_down_in, adapter_up_gate_input, adapter_up_rest, adapter_down_out, adapter_up_out):
    adapter_width = ADAPTER_COUNT * ADAPTER_RANK
    frozen = (block_norm_gain, gate_input_weight.astype(jnp.float32).reshape(MODEL_WIDTH, 2 * INNER_WIDTH), rest_weight.astype(jnp.float32), filter_taps_input, filter_taps_bc, step_bias, head_decay_rate, skip_weight, gated_norm_gain, output_weight.astype(jnp.float32))
    group_lens = lengths.reshape(N_DP, SEQ_GROUP)
    starts = (jnp.cumsum(group_lens, axis=1) - group_lens).astype(jnp.int32)
    position = jnp.arange(GROUP, dtype=jnp.int32)
    segment = (lax.optimization_barrier(jnp.sum((position[None, :, None] >= starts[:, None, :]).astype(jnp.int32), axis=2)) - 1).astype(jnp.int32)
    token_adapter = jnp.take_along_axis(sequence_adapter.reshape(N_DP, SEQ_GROUP), segment, axis=1).astype(jnp.int32)
    column_adapter_owner = jnp.arange(adapter_width, dtype=jnp.int32) // ADAPTER_RANK
    adapter_select_mask = (column_adapter_owner[None, None, :] == token_adapter[:, :, None]).astype(jnp.float32)

    def forward(resid_all, down_in_weight, up_gate_input_weight, up_rest_weight, down_out_weight, up_out_weight):
        adapter_params = (down_in_weight, up_gate_input_weight.reshape(adapter_width, 2, INNER_WIDTH), up_rest_weight, down_out_weight, up_out_weight)
        dealt = resid_all[perm].reshape(N_DP, GROUP, MODEL_WIDTH)

        def one_group(carried, items):
            return (carried, group_forward(items[0], items[1], items[2], adapter_params, frozen))
        final_carry, outputs = lax.scan(jax.checkpoint(one_group), jnp.float32(0.0), (dealt, segment, adapter_select_mask))
        return outputs.reshape(TOKENS, MODEL_WIDTH)[dealt_position]
    primal_values = tuple((numeric_array.astype(jnp.float32) for numeric_array in (tokens, adapter_down_in, adapter_up_gate_input, adapter_up_rest, adapter_down_out, adapter_up_out)))
    block_result, pull_back = jax.vjp(forward, *primal_values)
    gradients = pull_back(cotangent.astype(jnp.float32))
    return (block_result.astype(jnp.bfloat16), gradients[0].astype(jnp.bfloat16), gradients[1], gradients[2], gradients[3], gradients[4], gradients[5])
```

```python
from functools import partial

import jax
import jax.numpy as jnp
from jax import lax
from jax.experimental import pallas as pl
from jax.experimental.pallas import tpu as pltpu
from jax.sharding import PartitionSpec as P

MODEL_WIDTH = 1536
HEADDIM = 64
STATE = 128
LANES = 128
CHUNK = 128
BLOCK = 256
ADAPTER_RANK = 16
SEQ_GROUP = 4
REST_LOCAL = 2 * STATE + LANES

epsilon = 1e-05
LOG2E = 1.4426950408889634
VMEM_BYTES = 56 * 1024 * 1024
f32 = jnp.float32
bf16 = jnp.bfloat16

NN = (((1,), (0,)), ((), ()))
NT = (((1,), (1,)), ((), ()))
TN = (((0,), (0,)), ((), ()))


def mm(left, right, dims=NN):
    return lax.dot_general(left, right, dims, preferred_element_type=f32)


def params(count=1):
    return pltpu.CompilerParams(
        dimension_semantics=("arbitrary",) * count, vmem_limit_bytes=VMEM_BYTES
    )


def whole(shape):
    return pl.BlockSpec(shape, lambda *_: (0,) * len(shape))


def iota(shape, axis):
    return lax.broadcasted_iota(jnp.int32, shape, axis)


def pack_matrix(key_col, key_row):
    count = key_row.shape[1]
    rank = jnp.sum((key_col < key_row).astype(f32), axis=0, keepdims=True).astype(jnp.int32)
    return (iota((count, count), 0) == rank).astype(f32).astype(bf16)


def unpack_matrix(key_col, key_row):
    count = key_row.shape[1]
    rank = jnp.sum((key_row < key_col).astype(f32), axis=1, keepdims=True).astype(jnp.int32)
    return (iota((count, count), 1) == rank).astype(f32).astype(bf16)


def pack_kernel(key_col, key_row, first, second, first_out, second_out):
    select = pack_matrix(key_col[...], key_row[...])
    first_out[...] = mm(select, first[...]).astype(bf16)
    second_out[...] = mm(select, second[...]).astype(bf16)


def unpack_kernel(key_col, key_row, rows, rows_out):
    select = unpack_matrix(key_col[...], key_row[...])
    rows_out[...] = mm(select, rows[...]).astype(bf16)


def place_norm_kernel(key_col, key_row, rows, gain, rows_out, normed_out):
    select = unpack_matrix(key_col[...], key_row[...])
    resid = mm(select, rows[...])
    rows_out[...] = resid.astype(bf16)
    scale = lax.rsqrt(jnp.mean(resid * resid, axis=1, keepdims=True) + epsilon)
    normed_out[...] = (resid * scale * gain[...]).astype(bf16)


def simple_call(kernel, outs, flops, *args, scalars=0):
    vector = pl.BlockSpec(memory_space=pltpu.VMEM)
    scalar = pl.BlockSpec(memory_space=pltpu.SMEM)
    return pl.pallas_call(
        kernel,
        out_shape=outs,
        in_specs=[scalar] * scalars + [vector] * (len(args) - scalars),
        out_specs=jax.tree.map(lambda _: vector, outs),
        compiler_params=pltpu.CompilerParams(vmem_limit_bytes=VMEM_BYTES),
        cost_estimate=pl.CostEstimate(flops=flops, bytes_accessed=6_000_000, transcendentals=0),
    )(*args)


def segment_start(meta, position):
    begin = jnp.zeros_like(position)
    for k in range(1, SEQ_GROUP):
        begin = jnp.where(position >= meta[k], meta[k], begin)
    return begin


def adapter_mask(meta, first, rows):
    position = first + iota((rows, LANES), 0)
    owner = jnp.full((rows, LANES), meta[SEQ_GROUP], jnp.int32)
    for k in range(1, SEQ_GROUP):
        owner = jnp.where(position >= meta[k], meta[SEQ_GROUP + k], owner)
    return (iota((rows, LANES), 1) // ADAPTER_RANK == owner).astype(f32)


def cumulate(values):
    total = values
    step = 1
    while step < values.shape[0]:
        pad = jnp.zeros((step, values.shape[1]), f32)
        total = total + jnp.concatenate([pad, total[:-step]], axis=0)
        step *= 2
    return total


def cumulate_back(values):
    total = values
    step = 1
    while step < values.shape[0]:
        pad = jnp.zeros((step, values.shape[1]), f32)
        total = total + jnp.concatenate([total[step:], pad], axis=0)
        step *= 2
    return total


def sigmoid(values):
    return 1.0 / (1.0 + jnp.exp(-values))


def column(values, h):
    return jnp.broadcast_to(values[:, h : h + 1], (values.shape[0], LANES))


def decay_tables(dt, decay_rate):
    cumul = cumulate(dt * (-LOG2E * decay_rate))
    source = cumul - jnp.log(jnp.maximum(dt, 1e-37)) * LOG2E
    return cumul, source


def forward_kernel(
    meta,
    normed, w_x, w_rest, down_in, up_x, up_rest, taps, taps_bc, step_bias, decay_rate, skip,
    x_out, dx_out, y_out, state_out, bc_out, dbc_out, dt_out, sig_out, mid_out,
    conv_in, rest, state, from_state, scaled,
    *, heads, block,
):
    i = pl.program_id(0)
    inner = heads * HEADDIM
    per_block = block // CHUNK
    first = i * CHUNK

    @pl.when(i == 0)
    def _():
        conv_in[block : block + 8, :] = jnp.zeros((8, inner), f32)
        rest[block : block + 8, :] = jnp.zeros((8, REST_LOCAL), f32)
        state[...] = jnp.zeros_like(state)

    @pl.when(i % per_block == 0)
    def _():
        conv_in[0:8, :] = conv_in[block : block + 8, :]
        rest[0:8, :] = rest[block : block + 8, :]
        rows = normed[...]
        mid = (mm(rows, down_in[...]) * adapter_mask(meta, first, block)).astype(bf16)
        mid_out[...] = mid
        conv_in[8 : block + 8, :] = mm(rows, w_x[...]) + mm(mid, up_x[...])
        rest[8 : block + 8, :] = mm(rows, w_rest[...]) + mm(mid, up_rest[...])

    offset = pl.multiple_of((i % per_block) * CHUNK, CHUNK)
    window = pl.ds(offset, CHUNK + 8)
    position = first + iota((CHUNK, LANES), 0)
    begin = segment_start(meta, position)
    depth = position - begin
    same = [(depth >= k).astype(f32) for k in (1, 2, 3)]

    def conv(ext, tap):
        summed = tap[3:4] * ext[8:] + tap[4:5]
        for k in (1, 2, 3):
            summed = summed + tap[3 - k : 4 - k] * (ext[8 - k : 8 - k + CHUNK] * same[k - 1])
        sig = sigmoid(summed)
        act = summed * sig
        return act, sig + act * (1.0 - sig)

    b_act, b_slope = conv(rest[window, 0:STATE], taps_bc[:, 0:STATE])
    c_act, c_slope = conv(rest[window, STATE : 2 * STATE], taps_bc[:, STATE : 2 * STATE])
    b_mat = b_act.astype(bf16)
    c_mat = c_act.astype(bf16)
    bc_out[:, 0:STATE] = b_mat
    bc_out[:, STATE : 2 * STATE] = c_mat
    dbc_out[:, 0:STATE] = b_slope
    dbc_out[:, STATE : 2 * STATE] = c_slope
    step_pre = rest[window, 2 * STATE : REST_LOCAL][8:] + step_bias[...]
    dt = jnp.maximum(step_pre, 0.0) + jnp.log(1.0 + jnp.exp(-jnp.abs(step_pre)))
    small = jnp.exp(step_pre)
    dt = jnp.where(step_pre < -8.0, small * (1.0 - 0.5 * small), dt)
    dt_out[...] = dt
    sig_out[...] = sigmoid(step_pre)
    cumul, source = decay_tables(dt, decay_rate[...])
    source_rows = source.T
    total = cumul[CHUNK - 1 : CHUNK, :]
    s_pos = first + iota((CHUNK, CHUNK), 1)
    allowed = jnp.where((s_pos <= position) & (s_pos >= begin), 0.0, -1e30)
    scores = mm(c_mat, b_mat, NT)
    begin_last = segment_start(meta, first + CHUNK - 1)
    kept = jnp.where(begin_last < first, 1.0, 0.0)
    in_last = (position >= begin_last).astype(f32)
    carried = (begin < first).astype(f32)
    state_low = state[...].astype(bf16)
    state_out[...] = state_low
    from_state[...] = mm(c_mat, state_low)
    left = iota((CHUNK, LANES), 1) < HEADDIM
    left_row = left[0:1]
    for pair in range(heads // 2):
        h0, h1 = 2 * pair, 2 * pair + 1
        cols = slice(pair * LANES, (pair + 1) * LANES)
        act, slope = conv(conv_in[window, cols], taps[:, cols])
        x_low = act.astype(bf16)
        x_out[:, cols] = x_low
        dx_out[:, cols] = slope.astype(bf16)
        x = x_low.astype(f32)
        cum0, cum1 = column(cumul, h0), column(cumul, h1)
        m0 = jnp.exp2(cum0 - source_rows[h0 : h0 + 1] + allowed) * scores
        m1 = jnp.exp2(cum1 - source_rows[h1 : h1 + 1] + allowed) * scores
        weights = jnp.concatenate([m0.astype(bf16), m1.astype(bf16)], axis=1)
        x_split = jnp.concatenate(
            [jnp.where(left, x, 0.0).astype(bf16), jnp.where(left, 0.0, x).astype(bf16)], axis=0
        )
        inside = mm(weights, x_split)
        reach = jnp.exp2(jnp.where(left, cum0, cum1)) * carried
        y_out[:, cols] = inside + reach * from_state[:, cols] + skip[:, cols] * x
        total_pair = jnp.where(left_row, column(total, h0), column(total, h1))
        source_pair = jnp.where(left, column(source, h0), column(source, h1))
        coefficient = jnp.exp2(total_pair - source_pair) * in_last
        scaled[:, cols] = (x * coefficient).astype(bf16)
        state[:, cols] = state[:, cols] * (jnp.exp2(total_pair) * kept)
    state[...] += mm(b_mat, scaled[...], TN)


def forward_scan(meta, normed, w_x, w_rest, down_in, up_x, up_rest, taps, taps_bc, bias, decay, skip, heads):
    rows = normed.shape[0]
    inner = heads * HEADDIM
    block = min(BLOCK, rows)
    per_block = block // CHUNK
    chunk_rows = lambda width: pl.BlockSpec((CHUNK, width), lambda i, *_: (i, 0))
    block_rows = lambda width: pl.BlockSpec((block, width), lambda i, *_: (i // per_block, 0))
    outs = (
        jax.ShapeDtypeStruct((rows, inner), bf16),
        jax.ShapeDtypeStruct((rows, inner), bf16),
        jax.ShapeDtypeStruct((rows, inner), f32),
        jax.ShapeDtypeStruct((rows // CHUNK * STATE, inner), bf16),
        jax.ShapeDtypeStruct((rows, 2 * STATE), bf16),
        jax.ShapeDtypeStruct((rows, 2 * STATE), f32),
        jax.ShapeDtypeStruct((rows, LANES), f32),
        jax.ShapeDtypeStruct((rows, LANES), f32),
        jax.ShapeDtypeStruct((rows, LANES), bf16),
    )
    operands = (w_x, w_rest, down_in, up_x, up_rest, taps, taps_bc, bias, decay, skip)
    grid = pltpu.PrefetchScalarGridSpec(
        num_scalar_prefetch=1,
        grid=(rows // CHUNK,),
        in_specs=[block_rows(MODEL_WIDTH)] + [whole(a.shape) for a in operands],
        out_specs=[
            chunk_rows(inner), chunk_rows(inner), chunk_rows(inner), chunk_rows(inner),
            chunk_rows(2 * STATE), chunk_rows(2 * STATE), chunk_rows(LANES), chunk_rows(LANES),
            block_rows(LANES),
        ],
        scratch_shapes=[
            pltpu.VMEM((block + 8, inner), f32),
            pltpu.VMEM((block + 8, REST_LOCAL), f32),
            pltpu.VMEM((STATE, inner), f32),
            pltpu.VMEM((CHUNK, inner), f32),
            pltpu.VMEM((CHUNK, inner), bf16),
        ],
    )
    return pl.pallas_call(
        partial(forward_kernel, heads=heads, block=block),
        out_shape=outs,
        grid_spec=grid,
        compiler_params=params(),
        cost_estimate=pl.CostEstimate(
            flops=3 * rows * MODEL_WIDTH * inner, bytes_accessed=40_000_000, transcendentals=0
        ),
    )(meta, normed, *operands)


def gate_kernel(
    meta,
    normed, mid, scan_out, cotangent, w_gate, up_gate, w_out, down_out, up_out, gain,
    gate_out, weighted_out, gained_out, part_out, mid_part_out, gmid_out, stats_out,
    *, inner,
):
    block = normed.shape[0]
    first = pl.program_id(0) * block
    gate = mm(normed[...], w_gate[...]) + mm(mid[...], up_gate[...])
    gate_out[...] = gate
    gated = scan_out[...] * (gate * sigmoid(gate))
    square = jnp.sum(gated * gated, axis=1, keepdims=True)
    gained = (gated * gain[...]).astype(bf16)
    gained_out[...] = gained
    part_out[...] = mm(gained, w_out[...], NT).astype(bf16)
    mid_part_out[...] = mm(gained, down_out[...])
    gd = cotangent[...]
    gmid = (mm(gd, up_out[...], NT) * adapter_mask(meta, first, block)).astype(bf16)
    gmid_out[...] = gmid
    weighted = (mm(gd, w_out[...]) + mm(gmid, down_out[...], NT)) * gain[...]
    weighted_out[...] = weighted
    cross = jnp.sum(weighted * gated, axis=1, keepdims=True)
    lane = iota((block, LANES), 1)
    stats = jnp.where(lane == 0, square, jnp.where(lane == 1, cross, 0.0))
    stats_out[...] = stats.T[0:8, :]


def gate_stage(meta, normed, mid, scan_out, cotangent, w_gate, up_gate, w_out, down_out, up_out, gain):
    rows, inner = scan_out.shape
    block = min(BLOCK, rows)
    block_rows = lambda width: pl.BlockSpec((block, width), lambda i, *_: (i, 0))
    operands = (w_gate, up_gate, w_out, down_out, up_out, gain)
    outs = (
        jax.ShapeDtypeStruct((rows, inner), f32),
        jax.ShapeDtypeStruct((rows, inner), f32),
        jax.ShapeDtypeStruct((rows, inner), bf16),
        jax.ShapeDtypeStruct((rows, MODEL_WIDTH), bf16),
        jax.ShapeDtypeStruct((rows, LANES), f32),
        jax.ShapeDtypeStruct((rows, LANES), bf16),
        jax.ShapeDtypeStruct((8, rows), f32),
    )
    grid = pltpu.PrefetchScalarGridSpec(
        num_scalar_prefetch=1,
        grid=(rows // block,),
        in_specs=[block_rows(MODEL_WIDTH), block_rows(LANES), block_rows(inner), block_rows(MODEL_WIDTH)]
        + [whole(a.shape) for a in operands],
        out_specs=[
            block_rows(inner), block_rows(inner), block_rows(inner), block_rows(MODEL_WIDTH),
            block_rows(LANES), block_rows(LANES),
            pl.BlockSpec((8, block), lambda i, *_: (0, i)),
        ],
    )
    return pl.pallas_call(
        partial(gate_kernel, inner=inner),
        out_shape=outs,
        grid_spec=grid,
        compiler_params=params(),
        cost_estimate=pl.CostEstimate(
            flops=6 * rows * MODEL_WIDTH * inner, bytes_accessed=50_000_000, transcendentals=0
        ),
    )(meta, normed, mid, scan_out, cotangent, *operands)


def split_sum(values, indicator):
    high = values.astype(bf16)
    low = (values - high.astype(f32)).astype(bf16)
    return mm(high, indicator) + mm(low, indicator)


def backward_kernel(
    meta,
    scan_out, gate_pre, weighted, x_in, slope_in, bc_in, dbc_in, dt_in, sig_in, state_in, stats,
    gained, gmid, taps, taps_bc, decay_rate, skip, indicator,
    gz_out, grest_out, gdown_out,
    dstate, g_next, gbc_next, from_dstate, scaled, reached, product, source_product, row_product,
    *, heads, inner_all,
):
    i = pl.program_id(0)
    inner = heads * HEADDIM
    first = (pl.num_programs(0) - 1 - i) * CHUNK

    @pl.when(i == 0)
    def _():
        dstate[...] = jnp.zeros_like(dstate)
        g_next[...] = jnp.zeros_like(g_next)
        gbc_next[...] = jnp.zeros_like(gbc_next)
        gdown_out[...] = jnp.zeros_like(gdown_out)
        row_product[...] = jnp.zeros_like(row_product)

    s_pos = first + iota((CHUNK, LANES), 0)
    begin = segment_start(meta, s_pos)
    long_pos = first + iota((CHUNK + 8, LANES), 0)
    long_depth = long_pos - segment_start(meta, long_pos)
    same = [(long_depth >= k).astype(f32) for k in (1, 2, 3)]
    t_pos = first + iota((CHUNK, CHUNK), 1)
    t_begin = segment_start(meta, t_pos)
    allowed = jnp.where((s_pos <= t_pos) & (s_pos >= t_begin), 0.0, -1e30)
    begin_last = segment_start(meta, first + CHUNK - 1)
    kept = jnp.where(begin_last < first, 1.0, 0.0)
    in_last = (s_pos >= begin_last).astype(f32)
    carried = (begin < first).astype(f32)

    factor = lax.rsqrt(stats[0:1, :] * (1.0 / inner_all) + epsilon)
    pull = factor * factor * factor * stats[1:2, :] * (1.0 / inner_all)
    row_id = iota((LANES, CHUNK), 0)
    both = jnp.where(row_id == 0, factor, jnp.where(row_id == 1, pull, 0.0)).T
    factor_col, pull_col = column(both, 0), column(both, 1)

    gmid_scaled = (gmid[...].astype(f32) * factor_col).astype(bf16)
    gdown_out[...] += mm(gmid_scaled, gained[...], TN)

    dt = dt_in[...]
    sig = sig_in[...]
    cumul, source = decay_tables(dt, decay_rate[...])
    cumul_rows = cumul.T
    total = cumul[CHUNK - 1 : CHUNK, :]
    b_mat = bc_in[:, 0:STATE]
    c_mat = bc_in[:, STATE : 2 * STATE]
    scores = mm(b_mat, c_mat, NT)
    dstate_low = dstate[...].astype(bf16)
    from_dstate[...] = mm(b_mat, dstate_low)
    left = iota((CHUNK, LANES), 1) < HEADDIM
    left_row = left[0:1]
    gscores = jnp.zeros((CHUNK, CHUNK), f32)

    def conv_back(grad, later, tap):
        ext = jnp.concatenate([grad, later], axis=0)
        out = tap[3:4] * grad
        for k in (1, 2, 3):
            out = out + tap[3 - k : 4 - k] * (ext * same[k - 1])[k : k + CHUNK]
        return out

    for pair in range(heads // 2):
        h0, h1 = 2 * pair, 2 * pair + 1
        cols = slice(pair * LANES, (pair + 1) * LANES)
        gate = gate_pre[:, cols]
        y = scan_out[:, cols]
        gate_sig = sigmoid(gate)
        silu = gate * gate_sig
        ggated = weighted[:, cols] * factor_col - y * silu * pull_col
        gy_low = (ggated * silu).astype(bf16)
        gz_out[:, cols] = (ggated * y * (gate_sig + silu * (1.0 - gate_sig))).astype(bf16)
        gy = gy_low.astype(f32)
        gy_split = jnp.concatenate(
            [jnp.where(left, gy, 0.0).astype(bf16), jnp.where(left, 0.0, gy).astype(bf16)], axis=0
        )
        x_low = x_in[:, cols]
        x = x_low.astype(f32)
        dots = mm(x_low, gy_split, NT)
        src0, src1 = column(source, h0), column(source, h1)
        e0 = jnp.exp2(cumul_rows[h0 : h0 + 1] - src0 + allowed)
        e1 = jnp.exp2(cumul_rows[h1 : h1 + 1] - src1 + allowed)
        gscores = gscores + dots[:, 0:CHUNK] * e0 + dots[:, CHUNK:] * e1
        weights = jnp.concatenate([(e0 * scores).astype(bf16), (e1 * scores).astype(bf16)], axis=1)
        inside = mm(weights, gy_split)
        total_pair = jnp.where(left_row, column(total, h0), column(total, h1))
        coefficient = jnp.exp2(total_pair - jnp.where(left, src0, src1)) * in_last
        reach = jnp.exp2(jnp.where(left, column(cumul, h0), column(cumul, h1))) * carried
        outside = coefficient * from_dstate[:, cols]
        gx_scan = inside + outside
        skip_row = skip[:, cols]
        gx = gx_scan + skip_row * gy
        x_side = x * gx_scan
        source_product[:, cols] = x_side
        product[:, cols] = gy * (y - skip_row * x) - x_side
        scaled[:, cols] = (x * coefficient).astype(bf16)
        reached[:, cols] = (gy * reach).astype(bf16)
        keep_row = jnp.exp2(total_pair) * kept
        dstate_cols = dstate[:, cols]
        row_product[0:1, cols] = jnp.sum(x * outside, axis=0, keepdims=True) + keep_row * jnp.sum(
            dstate_cols * state_in[:, cols].astype(f32), axis=0, keepdims=True
        )
        dstate[:, cols] = dstate_cols * keep_row
        gconv = gx * slope_in[:, cols].astype(f32)
        gz_out[:, inner + pair * LANES : inner + (pair + 1) * LANES] = conv_back(
            gconv, g_next[:, cols], taps[:, cols]
        ).astype(bf16)
        g_next[:, cols] = gconv[0:8]

    gscores_low = gscores.astype(bf16)
    grad_b = mm(gscores_low, c_mat) + mm(scaled[...], dstate_low, NT)
    grad_c = mm(gscores_low, b_mat, TN) + mm(reached[...], state_in[...], NT)
    for part, grad in ((0, grad_b), (1, grad_c)):
        cols = slice(part * STATE, (part + 1) * STATE)
        gconv = grad * dbc_in[:, cols]
        grest_out[:, cols] = conv_back(gconv, gbc_next[:, cols], taps_bc[:, cols]).astype(bf16)
        gbc_next[:, cols] = gconv[0:8]
    dstate[...] += mm(c_mat, reached[...], TN)

    grad_cumul = split_sum(product[...], indicator[...])
    direct = split_sum(source_product[...], indicator[...])
    grad_total = split_sum(row_product[...], indicator[...])[0:1]
    grad_log = cumulate_back(grad_cumul) + grad_total
    ratio = jnp.where(dt > 1e-30, sig / jnp.maximum(dt, 1e-30), 1.0)
    grad_pre = direct * ratio - decay_rate[...] * grad_log * sig
    used = iota((CHUNK, LANES), 1) < heads
    grest_out[:, 2 * STATE : REST_LOCAL] = jnp.where(used, grad_pre, 0.0).astype(bf16)


def backward_scan(meta, scan_out, gate_pre, weighted, x_act, slope, bc, dbc, dt, sig, states, stats, gained, gmid, taps, taps_bc, decay, skip, indicator, heads, inner_all):
    rows, inner = scan_out.shape
    count = rows // CHUNK
    chunk_rows = lambda width: pl.BlockSpec((CHUNK, width), lambda i, *_: (count - 1 - i, 0))
    operands = (taps, taps_bc, decay, skip, indicator)
    streams = (scan_out, gate_pre, weighted, x_act, slope, bc, dbc, dt, sig, states)
    outs = (
        jax.ShapeDtypeStruct((rows, 2 * inner), bf16),
        jax.ShapeDtypeStruct((rows, REST_LOCAL), bf16),
        jax.ShapeDtypeStruct((LANES, inner), f32),
    )
    grid = pltpu.PrefetchScalarGridSpec(
        num_scalar_prefetch=1,
        grid=(count,),
        in_specs=[chunk_rows(a.shape[1]) for a in streams]
        + [pl.BlockSpec((8, CHUNK), lambda i, *_: (0, count - 1 - i))]
        + [chunk_rows(inner), chunk_rows(LANES)]
        + [whole(a.shape) for a in operands],
        out_specs=[chunk_rows(2 * inner), chunk_rows(REST_LOCAL), whole((LANES, inner))],
        scratch_shapes=[
            pltpu.VMEM((STATE, inner), f32),
            pltpu.VMEM((8, inner), f32),
            pltpu.VMEM((8, 2 * STATE), f32),
            pltpu.VMEM((CHUNK, inner), f32),
            pltpu.VMEM((CHUNK, inner), bf16),
            pltpu.VMEM((CHUNK, inner), bf16),
            pltpu.VMEM((CHUNK, inner), f32),
            pltpu.VMEM((CHUNK, inner), f32),
            pltpu.VMEM((8, inner), f32),
        ],
    )
    return pl.pallas_call(
        partial(backward_kernel, heads=heads, inner_all=inner_all),
        out_shape=outs,
        grid_spec=grid,
        compiler_params=params(),
        cost_estimate=pl.CostEstimate(
            flops=6 * rows * MODEL_WIDTH * inner, bytes_accessed=50_000_000, transcendentals=0
        ),
    )(meta, *streams, stats, gained, gmid, *operands)


def project_back_kernel(
    meta,
    gz, grest, normed, mid, w_gate, w_x, w_rest, down_in, up_gate, up_x, up_rest,
    grad_out, gdown_out, gup_out, gup_rest_out,
    *, inner,
):
    block = gz.shape[0]
    first = pl.program_id(0) * block

    @pl.when(pl.program_id(0) == 0)
    def _():
        gdown_out[...] = jnp.zeros_like(gdown_out)
        gup_out[...] = jnp.zeros_like(gup_out)
        gup_rest_out[...] = jnp.zeros_like(gup_rest_out)

    ggate = gz[:, 0:inner]
    gconv = gz[:, inner : 2 * inner]
    grest_rows = grest[...]
    gmid = mm(ggate, up_gate[...], NT) + mm(gconv, up_x[...], NT) + mm(grest_rows, up_rest[...], NT)
    gmid = (gmid * adapter_mask(meta, first, block)).astype(bf16)
    grad = mm(ggate, w_gate[...], NT) + mm(gconv, w_x[...], NT)
    grad = grad + mm(grest_rows, w_rest[...], NT) + mm(gmid, down_in[...], NT)
    grad_out[...] = grad.astype(bf16)
    mid_rows = mid[...]
    gdown_out[...] += mm(gmid, normed[...], TN)
    gup_out[...] += mm(mid_rows, gz[...], TN)
    gup_rest_out[...] += mm(mid_rows, grest_rows, TN)


def project_back(meta, gz, grest, normed, mid, w_gate, w_x, w_rest, down_in, up_gate, up_x, up_rest):
    rows = gz.shape[0]
    inner = gz.shape[1] // 2
    block = min(BLOCK, rows)
    block_rows = lambda width: pl.BlockSpec((block, width), lambda i, *_: (i, 0))
    operands = (w_gate, w_x, w_rest, down_in, up_gate, up_x, up_rest)
    outs = (
        jax.ShapeDtypeStruct((rows, MODEL_WIDTH), bf16),
        jax.ShapeDtypeStruct((LANES, MODEL_WIDTH), f32),
        jax.ShapeDtypeStruct((LANES, 2 * inner), f32),
        jax.ShapeDtypeStruct((LANES, REST_LOCAL), f32),
    )
    grid = pltpu.PrefetchScalarGridSpec(
        num_scalar_prefetch=1,
        grid=(rows // block,),
        in_specs=[block_rows(2 * inner), block_rows(REST_LOCAL), block_rows(MODEL_WIDTH), block_rows(LANES)]
        + [whole(a.shape) for a in operands],
        out_specs=[block_rows(MODEL_WIDTH)] + [whole(o.shape) for o in outs[1:]],
    )
    return pl.pallas_call(
        partial(project_back_kernel, inner=inner),
        out_shape=outs,
        grid_spec=grid,
        compiler_params=params(),
        cost_estimate=pl.CostEstimate(
            flops=5 * rows * MODEL_WIDTH * inner, bytes_accessed=40_000_000, transcendentals=0
        ),
    )(meta, gz, grest, normed, mid, *operands)


def output_kernel(
    meta, key_col, key_row, resid, own, other, mid_own, mid_other, stats, cotangent, up_out,
    sent_out, gup_out, *, inner_all,
):
    rows = resid.shape[0]
    row_id = iota((LANES, rows), 0)
    factor = lax.rsqrt(stats[0:1, :] * (1.0 / inner_all) + epsilon)
    factor_col = jnp.where(row_id == 0, factor, 0.0).T[:, 0:1]
    first = meta[2 * SEQ_GROUP]
    mid = (mid_own[...] + mid_other[...].astype(f32)) * factor_col
    mid = (mid * adapter_mask(meta, first, rows)).astype(bf16)
    summed = (own[...].astype(f32) + other[...].astype(f32)) * factor_col
    result = resid[...].astype(f32) + summed + mm(mid, up_out[...])
    select = pack_matrix(key_col[...], key_row[...])
    sent_out[...] = mm(select, result.astype(bf16)).astype(bf16)
    gup_out[...] = mm(mid, cotangent[...], TN)


def input_grad_kernel(key_col, key_row, resid, own, other, cotangent, gain, sent_out):
    values = resid[...].astype(f32)
    scale = lax.rsqrt(jnp.mean(values * values, axis=1, keepdims=True) + epsilon)
    weighted = (own[...].astype(f32) + other[...].astype(f32)) * gain[...]
    inner = jnp.mean(weighted * values, axis=1, keepdims=True)
    grad = scale * (weighted - values * (scale * scale * inner))
    result = cotangent[...].astype(f32) + grad
    select = pack_matrix(key_col[...], key_row[...])
    sent_out[...] = mm(select, result.astype(bf16)).astype(bf16)


def body(
    tokens,
    cotangent,
    lengths,
    sequence_adapter,
    perm,
    dealt_position,
    block_norm_gain,
    gate_input_weight,
    rest_weight,
    filter_taps_input,
    filter_taps_bc,
    step_bias,
    head_decay_rate,
    skip_weight,
    gated_norm_gain,
    output_weight,
    adapter_down_in,
    adapter_up_gate_input,
    adapter_up_rest,
    adapter_down_out,
    adapter_up_out,
):
    tensor_count = lax.axis_size("tensor")
    tok_dev = tokens.shape[0]
    group_rows = tok_dev * tensor_count
    heads = step_bias.shape[0]
    inner = heads * HEADDIM
    inner_all = inner * tensor_count
    dp_rank = lax.axis_index("dp")
    tensor_rank = lax.axis_index("tensor")
    swap = [(0, 1), (1, 0)]

    def deal(rows):
        return lax.all_to_all(rows, "dp", split_axis=0, concat_axis=0, tiled=True)

    def gather_rows(mine):
        if tensor_count != 2:
            return lax.all_gather(mine, "tensor", axis=0, tiled=True)
        other = lax.ppermute(mine, "tensor", swap)
        first = tensor_rank == 0
        return jnp.concatenate([jnp.where(first, mine, other), jnp.where(first, other, mine)])

    def own_rows(full, axis=0):
        return lax.dynamic_slice_in_dim(full, tensor_rank * tok_dev, tok_dev, axis)

    def reduce_rows(full):
        if tensor_count != 2:
            summed = lax.psum_scatter(full.astype(f32), "tensor", scatter_dimension=0, tiled=True)
            return summed, jnp.zeros_like(summed)
        theirs = lax.dynamic_slice_in_dim(full, (1 - tensor_rank) * tok_dev, tok_dev, 0)
        return own_rows(full), lax.ppermute(theirs.astype(bf16), "tensor", swap)

    group_lens = lax.dynamic_slice_in_dim(lengths, dp_rank * SEQ_GROUP, SEQ_GROUP)
    starts = jnp.cumsum(group_lens) - group_lens
    group_ids = lax.dynamic_slice_in_dim(sequence_adapter, dp_rank * SEQ_GROUP, SEQ_GROUP)
    meta = jnp.concatenate([starts, group_ids, (tensor_rank * tok_dev)[None]]).astype(jnp.int32)
    slot = jnp.arange(tok_dev, dtype=jnp.int32)
    given_key = (perm // group_rows) * tok_dev + slot
    dealt_key = (dealt_position // group_rows) * tok_dev + slot

    def keys(values):
        return values[:, None], values[None, :]

    token_rows = jax.ShapeDtypeStruct((tok_dev, MODEL_WIDTH), bf16)
    move_flops = 2 * tok_dev * tok_dev * MODEL_WIDTH
    gain_row = block_norm_gain[None, :]

    w_x = lax.all_gather(gate_input_weight[:, 1, :], "dp", axis=0, tiled=True)
    w_gate = lax.all_gather(gate_input_weight[:, 0, :], "dp", axis=0, tiled=True)
    w_out = lax.all_gather(output_weight.T, "dp", axis=0, tiled=True)
    rest_full = lax.all_gather(rest_weight, "dp", axis=0, tiled=True)
    dt_start = 2 * STATE + tensor_rank * heads

    def local_rest(matrix):
        steps = lax.dynamic_slice_in_dim(matrix, dt_start, heads, 1)
        return jnp.concatenate(
            [matrix[:, : 2 * STATE], jnp.pad(steps, ((0, 0), (0, LANES - heads)))], axis=1
        )

    w_rest = local_rest(rest_full)
    up_rest = local_rest(adapter_up_rest)
    up_gate = adapter_up_gate_input[:, 0, :]
    up_x = adapter_up_gate_input[:, 1, :]
    taps = jnp.pad(filter_taps_input, ((0, 3), (0, 0)))
    taps_bc = jnp.pad(filter_taps_bc, ((0, 3), (0, 0)))
    head_row = lambda values: jnp.pad(values, (0, LANES - heads))[None, :]
    bias_row, decay_row = head_row(step_bias), head_row(head_decay_rate)
    skip_row = jnp.repeat(skip_weight, HEADDIM)[None, :]
    indicator = (
        jnp.arange(inner)[:, None] // HEADDIM == jnp.arange(LANES)[None, :]
    ).astype(bf16)

    sent_tokens, sent_cotangent = simple_call(
        pack_kernel, (token_rows, token_rows), 2 * move_flops, *keys(dealt_position), tokens, cotangent
    )
    resid, normed_mine = simple_call(
        place_norm_kernel, (token_rows, token_rows), move_flops,
        *keys(given_key), deal(sent_tokens), gain_row,
    )
    normed = gather_rows(normed_mine)
    grad_mine = simple_call(
        unpack_kernel, token_rows, move_flops, *keys(given_key), deal(sent_cotangent)
    )
    grad_full = gather_rows(grad_mine)

    x_act, slope, scan_out, states, bc, dbc, dt, sig, mid_in = forward_scan(
        meta, normed, w_x, w_rest, adapter_down_in, up_x, up_rest, taps, taps_bc,
        bias_row, decay_row, skip_row, heads,
    )
    gate_pre, weighted, gained, part, mid_part, gmid, stats = gate_stage(
        meta, normed, mid_in, scan_out, grad_full, w_gate, up_gate, w_out, adapter_down_out,
        adapter_up_out, gated_norm_gain[None, :],
    )
    if tensor_count == 2:
        stats = stats + lax.ppermute(stats, "tensor", swap)
    else:
        stats = lax.psum(stats, "tensor")
    part_own, part_other = reduce_rows(part)
    mid_own, mid_other = reduce_rows(mid_part)
    sent_output, gup_out = simple_call(
        partial(output_kernel, inner_all=inner_all),
        (token_rows, jax.ShapeDtypeStruct((LANES, MODEL_WIDTH), f32)), 2 * move_flops,
        meta, *keys(perm), resid, part_own, part_other, mid_own, mid_other,
        own_rows(stats, 1), grad_mine, adapter_up_out, scalars=1,
    )
    output = simple_call(
        unpack_kernel, token_rows, move_flops, *keys(dealt_key), deal(sent_output)
    )

    gz, grest, gdown_out = backward_scan(
        meta, scan_out, gate_pre, weighted, x_act, slope, bc, dbc, dt, sig, states, stats,
        gained, gmid, taps, taps_bc, decay_row, skip_row, indicator, heads, inner_all,
    )
    grad_part, gdown_in, gup_zx, gup_rest = project_back(
        meta, gz, grest, normed, mid_in, w_gate, w_x, w_rest, adapter_down_in, up_gate, up_x, up_rest
    )
    grad_own, grad_other = reduce_rows(grad_part)
    sent_grad = simple_call(
        input_grad_kernel, token_rows, move_flops,
        *keys(perm), resid, grad_own, grad_other, grad_mine, gain_row,
    )
    input_grad = simple_call(
        unpack_kernel, token_rows, move_flops, *keys(dealt_key), deal(sent_grad)
    )

    rest_width = adapter_up_rest.shape[1]
    wide = jnp.concatenate(
        [gup_rest[:, : 2 * STATE], jnp.zeros((LANES, rest_width - 2 * STATE), f32)], axis=1
    )
    gup_rest = lax.dynamic_update_slice(
        wide, gup_rest[:, 2 * STATE : 2 * STATE + heads], (0, dt_start)
    )
    gdown_in, gup_rest, gup_out = lax.psum((gdown_in, gup_rest, gup_out), ("dp", "tensor"))
    gup_zx, gdown_out = lax.psum((gup_zx, gdown_out), "dp")
    return (
        output,
        input_grad,
        gdown_in.T,
        gup_zx.reshape(LANES, 2, inner),
        gup_rest,
        gdown_out.T,
        gup_out,
    )


def solution(mesh):
    placed = (
        P(("dp", "tensor"), None),
        P(("dp", "tensor"), None),
        P(),
        P(),
        P(("dp", "tensor")),
        P(("dp", "tensor")),
        P(),
        P("dp", None, "tensor"),
        P("dp", None),
        P(None, "tensor"),
        P(),
        P("tensor"),
        P("tensor"),
        P("tensor"),
        P("tensor"),
        P("tensor", "dp"),
        P(),
        P(None, None, "tensor"),
        P(),
        P("tensor", None),
        P(),
    )
    return jax.shard_map(
        body,
        mesh=mesh,
        in_specs=placed,
        out_specs=(
            P(("dp", "tensor"), None),
            P(("dp", "tensor"), None),
            P(),
            P(None, None, "tensor"),
            P(),
            P("tensor", None),
            P(),
        ),
        check_vma=False,
    )
```

```python
from functools import partial

import jax
import jax.numpy as jnp
from jax import lax
from jax.experimental import pallas as pl
from jax.experimental.pallas import tpu as pltpu
from jax.sharding import PartitionSpec as P

MODEL_WIDTH = 1536
HEADDIM = 64
STATE = 128
LANES = 128
CHUNK = 128
BLOCK = 256
ADAPTER_RANK = 16
SEQ_GROUP = 4
REST_LOCAL = 2 * STATE + LANES
META_HALF = 2 * SEQ_GROUP
META_RANK = META_HALF + 1
META_FIRST = META_HALF + 2
META_THEIRS = META_HALF + 3
COLUMNS = 512

epsilon = 1e-05
LOG2E = 1.4426950408889634
VMEM_BYTES = 56 * 1024 * 1024
f32 = jnp.float32
bf16 = jnp.bfloat16

NN = (((1,), (0,)), ((), ()))
NT = (((1,), (1,)), ((), ()))
TN = (((0,), (0,)), ((), ()))


def mm(left, right, dims=NN):
    return lax.dot_general(left, right, dims, preferred_element_type=f32)


def params(count=1):
    return pltpu.CompilerParams(
        dimension_semantics=("arbitrary",) * count, vmem_limit_bytes=VMEM_BYTES
    )


def whole(shape):
    return pl.BlockSpec(shape, lambda *_: (0,) * len(shape))


def iota(shape, axis):
    return lax.broadcasted_iota(jnp.int32, shape, axis)


def pack_matrix(key_col, key_row):
    count = key_row.shape[1]
    rank = jnp.sum((key_col < key_row).astype(f32), axis=0, keepdims=True).astype(jnp.int32)
    return (iota((count, count), 0) == rank).astype(f32).astype(bf16)


def unpack_matrix(key_col, key_row):
    count = key_row.shape[1]
    rank = jnp.sum((key_row < key_col).astype(f32), axis=1, keepdims=True).astype(jnp.int32)
    return (iota((count, count), 1) == rank).astype(f32).astype(bf16)


def pack_kernel(key_col, key_row, first, second, first_out, second_out):
    select = pack_matrix(key_col[...], key_row[...])
    first_out[...] = mm(select, first[...]).astype(bf16)
    second_out[...] = mm(select, second[...]).astype(bf16)


def unpack_kernel(key_col, key_row, rows, rows_out):
    select = unpack_matrix(key_col[...], key_row[...])
    rows_out[...] = mm(select, rows[...]).astype(bf16)


def place_norm_kernel(key_col, key_row, rows, gain, rows_out, normed_out):
    select = unpack_matrix(key_col[...], key_row[...])
    resid = mm(select, rows[...])
    rows_out[...] = resid.astype(bf16)
    scale = lax.rsqrt(jnp.mean(resid * resid, axis=1, keepdims=True) + epsilon)
    normed_out[...] = (resid * scale * gain[...]).astype(bf16)


def simple_call(kernel, outs, flops, *args, scalars=0):
    vector = pl.BlockSpec(memory_space=pltpu.VMEM)
    scalar = pl.BlockSpec(memory_space=pltpu.SMEM)
    return pl.pallas_call(
        kernel,
        out_shape=outs,
        in_specs=[scalar] * scalars + [vector] * (len(args) - scalars),
        out_specs=jax.tree.map(lambda _: vector, outs),
        compiler_params=pltpu.CompilerParams(vmem_limit_bytes=VMEM_BYTES),
        cost_estimate=pl.CostEstimate(flops=flops, bytes_accessed=1_000_000, transcendentals=0),
    )(*args)


def segment_start(meta, position):
    begin = jnp.zeros_like(position)
    for k in range(1, SEQ_GROUP):
        begin = jnp.where(position >= meta[k], meta[k], begin)
    return begin


def row_specs(block, width, place):
    def spec(side):
        def index(i, meta):
            half = meta[META_HALF]
            return (jnp.clip(place(i, meta) - meta[side] * half, 0, half - 1), 0)

        return pl.BlockSpec((block, width), index)

    return [spec(META_RANK), spec(META_THEIRS)]


def pick_rows(meta, place, mine, other):
    own = place // meta[META_HALF] == meta[META_RANK]
    return jnp.where(own, mine[...], other[...])


def adapter_mask(meta, first, rows):
    position = first + iota((rows, LANES), 0)
    owner = jnp.full((rows, LANES), meta[SEQ_GROUP], jnp.int32)
    for k in range(1, SEQ_GROUP):
        owner = jnp.where(position >= meta[k], meta[SEQ_GROUP + k], owner)
    return (iota((rows, LANES), 1) // ADAPTER_RANK == owner).astype(f32)


def cumulate(values):
    total = values
    step = 1
    while step < values.shape[0]:
        pad = jnp.zeros((step, values.shape[1]), f32)
        total = total + jnp.concatenate([pad, total[:-step]], axis=0)
        step *= 2
    return total


def cumulate_back(values):
    total = values
    step = 1
    while step < values.shape[0]:
        pad = jnp.zeros((step, values.shape[1]), f32)
        total = total + jnp.concatenate([total[step:], pad], axis=0)
        step *= 2
    return total


def sigmoid(values):
    return 0.5 * jnp.tanh(0.5 * values) + 0.5


def column(values, h):
    return jnp.broadcast_to(values[:, h : h + 1], (values.shape[0], LANES))


def decay_tables(dt, decay_rate):
    cumul = cumulate(dt * (-LOG2E * decay_rate))
    source = cumul - jnp.log(jnp.maximum(dt, 1e-37)) * LOG2E
    return cumul, source


def forward_kernel(
    meta,
    mine, other, w_in, down_in, up_x, up_rest, up_gate, taps, taps_bc, step_bias, decay_rate, skip, gain,
    x_out, dx_out, y_out, gate_out, gained_out, state_out, bc_out, dbc_out, dt_out, sig_out, mid_out,
    square_out,
    conv_in, rest, gate_pre, state, from_state, scaled,
    *, heads, block,
):
    i = pl.program_id(0)
    inner = heads * HEADDIM
    per_block = block // CHUNK
    first = i * CHUNK

    @pl.when(i == 0)
    def _():
        conv_in[block : block + 8, :] = jnp.zeros((8, inner), f32)
        rest[block : block + 8, :] = jnp.zeros((8, REST_LOCAL), f32)
        state[...] = jnp.zeros_like(state)

    @pl.when(i % per_block == 0)
    def _():
        conv_in[0:8, :] = conv_in[block : block + 8, :]
        rest[0:8, :] = rest[block : block + 8, :]
        rows = pick_rows(meta, i // per_block, mine, other)
        mid = (mm(rows, down_in[...]) * adapter_mask(meta, first, block)).astype(bf16)
        mid_out[...] = mid
        conv_in[8 : block + 8, :] = mm(rows, w_in[:, 0:inner]) + mm(mid, up_x[...])
        gate_pre[...] = mm(rows, w_in[:, inner : 2 * inner]) + mm(mid, up_gate[...])
        rest[8 : block + 8, :] = mm(rows, w_in[:, 2 * inner :]) + mm(mid, up_rest[...])

    offset = pl.multiple_of((i % per_block) * CHUNK, CHUNK)
    window = pl.ds(offset, CHUNK + 8)
    position = first + iota((CHUNK, LANES), 0)
    begin = segment_start(meta, position)
    depth = position - begin
    same = [(depth >= k).astype(f32) for k in (1, 2, 3)]

    def conv(ext, tap):
        summed = tap[3:4] * ext[8:] + tap[4:5]
        for k in (1, 2, 3):
            summed = summed + tap[3 - k : 4 - k] * (ext[8 - k : 8 - k + CHUNK] * same[k - 1])
        sig = sigmoid(summed)
        act = summed * sig
        return act, sig + act * (1.0 - sig)

    b_act, b_slope = conv(rest[window, 0:STATE], taps_bc[:, 0:STATE])
    c_act, c_slope = conv(rest[window, STATE : 2 * STATE], taps_bc[:, STATE : 2 * STATE])
    b_mat = b_act.astype(bf16)
    c_mat = c_act.astype(bf16)
    bc_out[:, 0:STATE] = b_mat
    bc_out[:, STATE : 2 * STATE] = c_mat
    dbc_out[:, 0:STATE] = b_slope
    dbc_out[:, STATE : 2 * STATE] = c_slope
    step_pre = rest[window, 2 * STATE : REST_LOCAL][8:] + step_bias[...]
    dt = jnp.maximum(step_pre, 0.0) + jnp.log(1.0 + jnp.exp(-jnp.abs(step_pre)))
    small = jnp.exp(step_pre)
    dt = jnp.where(step_pre < -8.0, small * (1.0 - 0.5 * small), dt)
    dt_out[...] = dt
    sig_out[...] = sigmoid(step_pre)
    cumul, source = decay_tables(dt, decay_rate[...])
    source_rows = source.T
    total = cumul[CHUNK - 1 : CHUNK, :]
    s_pos = first + iota((CHUNK, CHUNK), 1)
    allowed = jnp.where((s_pos <= position) & (s_pos >= begin), 0.0, -1e30)
    scores = mm(c_mat, b_mat, NT)
    begin_last = segment_start(meta, first + CHUNK - 1)
    kept = jnp.where(begin_last < first, 1.0, 0.0)
    in_last = (position >= begin_last).astype(f32)
    carried = (begin < first).astype(f32)
    state_low = state[...].astype(bf16)
    state_out[...] = state_low
    from_state[...] = mm(c_mat, state_low)
    left = iota((CHUNK, LANES), 1) < HEADDIM
    left_row = left[0:1]
    square = jnp.zeros((CHUNK, LANES), f32)
    for pair in range(heads // 2):
        h0, h1 = 2 * pair, 2 * pair + 1
        cols = slice(pair * LANES, (pair + 1) * LANES)
        act, slope = conv(conv_in[window, cols], taps[:, cols])
        x_low = act.astype(bf16)
        x_out[:, cols] = x_low
        dx_out[:, cols] = slope.astype(bf16)
        x = x_low.astype(f32)
        cum0, cum1 = column(cumul, h0), column(cumul, h1)
        m0 = jnp.exp2(cum0 - source_rows[h0 : h0 + 1] + allowed) * scores
        m1 = jnp.exp2(cum1 - source_rows[h1 : h1 + 1] + allowed) * scores
        weights = jnp.concatenate([m0.astype(bf16), m1.astype(bf16)], axis=1)
        x_split = jnp.concatenate(
            [jnp.where(left, x, 0.0).astype(bf16), jnp.where(left, 0.0, x).astype(bf16)], axis=0
        )
        inside = mm(weights, x_split)
        reach = jnp.exp2(jnp.where(left, cum0, cum1)) * carried
        y = inside + reach * from_state[:, cols] + skip[:, cols] * x
        y_out[:, cols] = y
        gate = gate_pre[pl.ds(offset, CHUNK), cols]
        gate_out[:, cols] = gate
        gated = y * (gate * sigmoid(gate))
        square = square + gated * gated
        gained_out[:, cols] = (gated * gain[:, cols]).astype(bf16)
        total_pair = jnp.where(left_row, column(total, h0), column(total, h1))
        source_pair = jnp.where(left, column(source, h0), column(source, h1))
        coefficient = jnp.exp2(total_pair - source_pair) * in_last
        scaled[:, cols] = (x * coefficient).astype(bf16)
        state[:, cols] = state[:, cols] * (jnp.exp2(total_pair) * kept)
    state[...] += mm(b_mat, scaled[...], TN)
    square_out[...] = jnp.sum(square.T, axis=0, keepdims=True)


def forward_scan(meta, normed, w_in, down_in, up_x, up_rest, up_gate, taps, taps_bc, bias, decay, skip, gain, heads, rows, block):
    inner = heads * HEADDIM
    per_block = block // CHUNK
    chunk_rows = lambda width: pl.BlockSpec((CHUNK, width), lambda i, *_: (i, 0))
    block_rows = lambda width: pl.BlockSpec((block, width), lambda i, *_: (i // per_block, 0))
    outs = (
        jax.ShapeDtypeStruct((rows, inner), bf16),
        jax.ShapeDtypeStruct((rows, inner), bf16),
        jax.ShapeDtypeStruct((rows, inner), f32),
        jax.ShapeDtypeStruct((rows, inner), f32),
        jax.ShapeDtypeStruct((rows, inner), bf16),
        jax.ShapeDtypeStruct((rows // CHUNK * STATE, inner), bf16),
        jax.ShapeDtypeStruct((rows, 2 * STATE), bf16),
        jax.ShapeDtypeStruct((rows, 2 * STATE), f32),
        jax.ShapeDtypeStruct((rows, LANES), f32),
        jax.ShapeDtypeStruct((rows, LANES), f32),
        jax.ShapeDtypeStruct((rows, LANES), bf16),
        jax.ShapeDtypeStruct((1, rows), f32),
    )
    operands = (w_in, down_in, up_x, up_rest, up_gate, taps, taps_bc, bias, decay, skip, gain)
    grid = pltpu.PrefetchScalarGridSpec(
        num_scalar_prefetch=1,
        grid=(rows // CHUNK,),
        in_specs=row_specs(block, MODEL_WIDTH, lambda i, meta: i // per_block)
        + [whole(a.shape) for a in operands],
        out_specs=[
            chunk_rows(inner), chunk_rows(inner), chunk_rows(inner), chunk_rows(inner),
            chunk_rows(inner), chunk_rows(inner),
            chunk_rows(2 * STATE), chunk_rows(2 * STATE), chunk_rows(LANES), chunk_rows(LANES),
            block_rows(LANES), pl.BlockSpec((1, CHUNK), lambda i, *_: (0, i)),
        ],
        scratch_shapes=[
            pltpu.VMEM((block + 8, inner), f32),
            pltpu.VMEM((block + 8, REST_LOCAL), f32),
            pltpu.VMEM((block, inner), f32),
            pltpu.VMEM((STATE, inner), f32),
            pltpu.VMEM((CHUNK, inner), f32),
            pltpu.VMEM((CHUNK, inner), bf16),
        ],
    )
    return pl.pallas_call(
        partial(forward_kernel, heads=heads, block=block),
        out_shape=outs,
        grid_spec=grid,
        compiler_params=params(),
        cost_estimate=pl.CostEstimate(
            flops=5 * rows * MODEL_WIDTH * inner, bytes_accessed=50_000_000, transcendentals=0
        ),
    )(meta, *normed, *operands)


def out_grad_kernel(
    meta,
    gd_mine, gd_other, gained, square, w_out, down_out, up_out, gain,
    weighted_out, gmid_out, stats_out,
    gd, cross,
    *, pairwise,
):
    step = pl.program_id(0)
    rows = gd.shape[0]

    @pl.when(step == 0)
    def _():
        if pairwise:
            tokens = gd_mine.shape[0]
            gd[pl.ds(pl.multiple_of(meta[META_FIRST], LANES), tokens), :] = gd_mine[...]
            gd[pl.ds(pl.multiple_of(rows - tokens - meta[META_FIRST], LANES), tokens), :] = gd_other[...]
        else:
            gd[...] = gd_mine[...]
        gmid = mm(gd[...], up_out[...], NT) * adapter_mask(meta, 0, rows)
        gmid_out[...] = gmid.astype(bf16)
        cross[...] = jnp.zeros_like(cross)

    grad = mm(gd[...], w_out[...]) + mm(gmid_out[...], down_out[...], NT)
    weighted_out[...] = grad * gain[...]
    product = grad * gained[...].astype(f32)
    total = cross[...]
    for tile in range(product.shape[1] // LANES):
        total = total + product[:, tile * LANES : (tile + 1) * LANES]
    cross[...] = total

    @pl.when(step == pl.num_programs(0) - 1)
    def _():
        row = jnp.sum(cross[...].T, axis=0, keepdims=True)
        stats_out[...] = jnp.where(iota((8, rows), 0) == 0, square[...], row)


def out_grad(meta, cotangent, gained, square, w_out, down_out, up_out, gain, pairwise):
    rows, inner = gained.shape
    width = 4 * LANES if inner % (4 * LANES) == 0 else LANES
    columns = lambda height: pl.BlockSpec((height, width), lambda i, *_: (0, i))
    outs = (
        jax.ShapeDtypeStruct((rows, inner), f32),
        jax.ShapeDtypeStruct((rows, LANES), bf16),
        jax.ShapeDtypeStruct((8, rows), f32),
    )
    grid = pltpu.PrefetchScalarGridSpec(
        num_scalar_prefetch=1,
        grid=(inner // width,),
        in_specs=[
            whole(cotangent[0].shape), whole(cotangent[1].shape), columns(rows), whole(square.shape),
            columns(MODEL_WIDTH), pl.BlockSpec((width, LANES), lambda i, *_: (i, 0)),
            whole(up_out.shape), columns(1),
        ],
        out_specs=[columns(rows), whole(outs[1].shape), whole(outs[2].shape)],
        scratch_shapes=[pltpu.VMEM((rows, MODEL_WIDTH), bf16), pltpu.VMEM((rows, LANES), f32)],
    )
    return pl.pallas_call(
        partial(out_grad_kernel, pairwise=pairwise),
        out_shape=outs,
        grid_spec=grid,
        compiler_params=params(),
        cost_estimate=pl.CostEstimate(
            flops=2 * rows * MODEL_WIDTH * inner, bytes_accessed=20_000_000, transcendentals=0
        ),
    )(meta, *cotangent, gained, square, w_out, down_out, up_out, gain)


def halves(meta_rows, width):
    theirs = pl.BlockSpec((meta_rows, width), lambda i, meta: (meta[META_THEIRS], 0))
    own = pl.BlockSpec((meta_rows, width), lambda i, meta: (meta[META_RANK], 0))
    return theirs, own


def out_project_kernel(meta, theirs, own, w_out, down_out, sent_out, kept_out):
    step = pl.program_id(0)
    width = w_out.shape[0]
    columns = pl.ds(pl.multiple_of(step * width, LANES), width)
    sent_out[:, columns] = mm(theirs[...], w_out[...], NT).astype(bf16)
    kept_out[:, columns] = mm(own[...], w_out[...], NT).astype(bf16)

    @pl.when(step == 0)
    def _():
        sent_out[:, MODEL_WIDTH:] = mm(theirs[...], down_out[...]).astype(bf16)
        kept_out[:, MODEL_WIDTH:] = mm(own[...], down_out[...]).astype(bf16)


def out_project(meta, gained, w_out, down_out, half_rows):
    inner = gained.shape[1]
    out = jax.ShapeDtypeStruct((half_rows, MODEL_WIDTH + LANES), bf16)
    grid = pltpu.PrefetchScalarGridSpec(
        num_scalar_prefetch=1,
        grid=(MODEL_WIDTH // COLUMNS,),
        in_specs=[
            *halves(half_rows, inner),
            pl.BlockSpec((COLUMNS, inner), lambda i, *_: (i, 0)),
            whole(down_out.shape),
        ],
        out_specs=[whole(out.shape)] * 2,
    )
    return pl.pallas_call(
        out_project_kernel,
        out_shape=(out, out),
        grid_spec=grid,
        compiler_params=params(),
        cost_estimate=pl.CostEstimate(
            flops=4 * half_rows * MODEL_WIDTH * inner, bytes_accessed=15_000_000, transcendentals=0
        ),
    )(meta, gained, gained, w_out, down_out)


def split_sum(values, indicator):
    high = values.astype(bf16)
    low = (values - high.astype(f32)).astype(bf16)
    return mm(high, indicator) + mm(low, indicator)


def backward_kernel(
    meta,
    scan_out, gate_pre, weighted, x_in, slope_in, bc_in, dbc_in, dt_in, sig_in, state_in, stats,
    taps, taps_bc, decay_rate, skip, indicator,
    gz_out, grest_out,
    dstate, g_next, gbc_next, from_dstate, scaled, reached, product, source_product,
    *, heads, inner_all,
):
    i = pl.program_id(0)
    inner = heads * HEADDIM
    first = (pl.num_programs(0) - 1 - i) * CHUNK

    @pl.when(i == 0)
    def _():
        dstate[...] = jnp.zeros_like(dstate)
        g_next[...] = jnp.zeros_like(g_next)
        gbc_next[...] = jnp.zeros_like(gbc_next)
        product[CHUNK:, :] = jnp.zeros((8, inner), f32)

    s_pos = first + iota((CHUNK, LANES), 0)
    begin = segment_start(meta, s_pos)
    long_pos = first + iota((CHUNK + 8, LANES), 0)
    long_depth = long_pos - segment_start(meta, long_pos)
    same = [(long_depth >= k).astype(f32) for k in (1, 2, 3)]
    t_pos = first + iota((CHUNK, CHUNK), 1)
    t_begin = segment_start(meta, t_pos)
    allowed = jnp.where((s_pos <= t_pos) & (s_pos >= t_begin), 0.0, -1e30)
    begin_last = segment_start(meta, first + CHUNK - 1)
    kept = jnp.where(begin_last < first, 1.0, 0.0)
    in_last = (s_pos >= begin_last).astype(f32)
    carried = (begin < first).astype(f32)

    factor = lax.rsqrt(stats[0:1, :] * (1.0 / inner_all) + epsilon)
    pull = factor * factor * factor * stats[1:2, :] * (1.0 / inner_all)
    row_id = iota((LANES, CHUNK), 0)
    both = jnp.where(row_id == 0, factor, jnp.where(row_id == 1, pull, 0.0)).T
    factor_col, pull_col = column(both, 0), column(both, 1)

    dt = dt_in[...]
    sig = sig_in[...]
    cumul, source = decay_tables(dt, decay_rate[...])
    cumul_rows = cumul.T
    total = cumul[CHUNK - 1 : CHUNK, :]
    b_mat = bc_in[:, 0:STATE]
    c_mat = bc_in[:, STATE : 2 * STATE]
    scores = mm(b_mat, c_mat, NT)
    dstate_low = dstate[...].astype(bf16)
    from_dstate[...] = mm(b_mat, dstate_low)
    left = iota((CHUNK, LANES), 1) < HEADDIM
    left_row = left[0:1]
    gscores = jnp.zeros((CHUNK, CHUNK), f32)

    def conv_back(grad, later, tap):
        ext = jnp.concatenate([grad, later], axis=0)
        out = tap[3:4] * grad
        for k in (1, 2, 3):
            out = out + tap[3 - k : 4 - k] * (ext * same[k - 1])[k : k + CHUNK]
        return out

    for pair in range(heads // 2):
        h0, h1 = 2 * pair, 2 * pair + 1
        cols = slice(pair * LANES, (pair + 1) * LANES)
        gate = gate_pre[:, cols]
        y = scan_out[:, cols]
        gate_sig = sigmoid(gate)
        silu = gate * gate_sig
        ggated = weighted[:, cols] * factor_col - y * silu * pull_col
        gy_low = (ggated * silu).astype(bf16)
        gz_out[:, cols] = (ggated * y * (gate_sig + silu * (1.0 - gate_sig))).astype(bf16)
        gy = gy_low.astype(f32)
        gy_split = jnp.concatenate(
            [jnp.where(left, gy, 0.0).astype(bf16), jnp.where(left, 0.0, gy).astype(bf16)], axis=0
        )
        x_low = x_in[:, cols]
        x = x_low.astype(f32)
        dots = mm(x_low, gy_split, NT)
        src0, src1 = column(source, h0), column(source, h1)
        e0 = jnp.exp2(cumul_rows[h0 : h0 + 1] - src0 + allowed)
        e1 = jnp.exp2(cumul_rows[h1 : h1 + 1] - src1 + allowed)
        gscores = gscores + dots[:, 0:CHUNK] * e0 + dots[:, CHUNK:] * e1
        weights = jnp.concatenate([(e0 * scores).astype(bf16), (e1 * scores).astype(bf16)], axis=1)
        inside = mm(weights, gy_split)
        total_pair = jnp.where(left_row, column(total, h0), column(total, h1))
        coefficient = jnp.exp2(total_pair - jnp.where(left, src0, src1)) * in_last
        reach = jnp.exp2(jnp.where(left, column(cumul, h0), column(cumul, h1))) * carried
        outside = coefficient * from_dstate[:, cols]
        gx_scan = inside + outside
        skip_row = skip[:, cols]
        gx = gx_scan + skip_row * gy
        x_side = x * gx_scan
        source_product[:, cols] = x_side.astype(bf16)
        product[0:CHUNK, cols] = gy * (y - skip_row * x) - x_side
        scaled[:, cols] = (x * coefficient).astype(bf16)
        reached[:, cols] = (gy * reach).astype(bf16)
        keep_row = jnp.exp2(total_pair) * kept
        dstate_cols = dstate[:, cols]
        product[CHUNK : CHUNK + 1, cols] = jnp.sum(x * outside, axis=0, keepdims=True) + keep_row * jnp.sum(
            dstate_cols * state_in[:, cols].astype(f32), axis=0, keepdims=True
        )
        dstate[:, cols] = dstate_cols * keep_row
        gconv = gx * slope_in[:, cols].astype(f32)
        gz_out[:, inner + pair * LANES : inner + (pair + 1) * LANES] = conv_back(
            gconv, g_next[:, cols], taps[:, cols]
        ).astype(bf16)
        g_next[:, cols] = gconv[0:8]

    gscores_low = gscores.astype(bf16)
    grad_b = mm(gscores_low, c_mat) + mm(scaled[...], dstate_low, NT)
    grad_c = mm(gscores_low, b_mat, TN) + mm(reached[...], state_in[...], NT)
    for part, grad in ((0, grad_b), (1, grad_c)):
        cols = slice(part * STATE, (part + 1) * STATE)
        gconv = grad * dbc_in[:, cols]
        grest_out[:, cols] = conv_back(gconv, gbc_next[:, cols], taps_bc[:, cols]).astype(bf16)
        gbc_next[:, cols] = gconv[0:8]
    dstate[...] += mm(c_mat, reached[...], TN)

    sums = split_sum(product[...], indicator[...])
    direct = mm(source_product[...], indicator[...])
    grad_log = cumulate_back(sums[0:CHUNK]) + sums[CHUNK : CHUNK + 1]
    ratio = jnp.where(dt > 1e-30, sig / jnp.maximum(dt, 1e-30), 1.0)
    grad_pre = direct * ratio - decay_rate[...] * grad_log * sig
    used = iota((CHUNK, LANES), 1) < heads
    grest_out[:, 2 * STATE : REST_LOCAL] = jnp.where(used, grad_pre, 0.0).astype(bf16)


def backward_scan(meta, scan_out, gate_pre, weighted, x_act, slope, bc, dbc, dt, sig, states, stats, taps, taps_bc, decay, skip, indicator, heads, inner_all):
    rows, inner = scan_out.shape
    count = rows // CHUNK
    chunk_rows = lambda width: pl.BlockSpec((CHUNK, width), lambda i, *_: (count - 1 - i, 0))
    operands = (taps, taps_bc, decay, skip, indicator)
    streams = (scan_out, gate_pre, weighted, x_act, slope, bc, dbc, dt, sig, states)
    outs = (
        jax.ShapeDtypeStruct((rows, 2 * inner), bf16),
        jax.ShapeDtypeStruct((rows, REST_LOCAL), bf16),
    )
    grid = pltpu.PrefetchScalarGridSpec(
        num_scalar_prefetch=1,
        grid=(count,),
        in_specs=[chunk_rows(a.shape[1]) for a in streams]
        + [pl.BlockSpec((8, CHUNK), lambda i, *_: (0, count - 1 - i))]
        + [whole(a.shape) for a in operands],
        out_specs=[chunk_rows(2 * inner), chunk_rows(REST_LOCAL)],
        scratch_shapes=[
            pltpu.VMEM((STATE, inner), f32),
            pltpu.VMEM((8, inner), f32),
            pltpu.VMEM((8, 2 * STATE), f32),
            pltpu.VMEM((CHUNK, inner), f32),
            pltpu.VMEM((CHUNK, inner), bf16),
            pltpu.VMEM((CHUNK, inner), bf16),
            pltpu.VMEM((CHUNK + 8, inner), f32),
            pltpu.VMEM((CHUNK, inner), bf16),
        ],
    )
    return pl.pallas_call(
        partial(backward_kernel, heads=heads, inner_all=inner_all),
        out_shape=outs,
        grid_spec=grid,
        compiler_params=params(),
        cost_estimate=pl.CostEstimate(
            flops=6 * rows * MODEL_WIDTH * inner, bytes_accessed=50_000_000, transcendentals=0
        ),
    )(meta, *streams, stats, *operands)


def turn_tiles(out, first, values):
    for tile in range(values.shape[1] // LANES):
        out[:, first + tile * LANES : first + (tile + 1) * LANES] = values[
            :, tile * LANES : (tile + 1) * LANES
        ].T


def adapter_back_kernel(
    meta,
    gz, grest, normed_mine, normed_other, mid, gained, gmid_out_rows, stats, gup_out, up_gate, up_x, up_rest,
    gmid_out, grads, down_in, down_out,
    *, inner, inner_all,
):
    block = gz.shape[0]
    place = pl.program_id(0)
    rest_at = 2 * MODEL_WIDTH
    zx_at = rest_at + REST_LOCAL
    out_at = zx_at + 2 * inner

    @pl.when(place == 0)
    def _():
        grads[...] = jnp.zeros_like(grads)
        grads[:, MODEL_WIDTH:rest_at] = gup_out[...]
        down_in[...] = jnp.zeros_like(down_in)
        down_out[...] = jnp.zeros_like(down_out)

    grest_rows = grest[...]
    gmid = mm(gz[:, 0:inner], up_gate[...], NT) + mm(gz[:, inner : 2 * inner], up_x[...], NT)
    gmid = gmid + mm(grest_rows, up_rest[...], NT)
    gmid = (gmid * adapter_mask(meta, place * block, block)).astype(bf16)
    gmid_out[...] = gmid
    mid_rows = mid[...]
    down_in[...] += mm(gmid, pick_rows(meta, place, normed_mine, normed_other), TN)
    grads[:, zx_at:out_at] += mm(mid_rows, gz[...], TN)
    grads[:, rest_at:zx_at] += mm(mid_rows, grest_rows, TN)
    factor = lax.rsqrt(stats[0:1, :] * (1.0 / inner_all) + epsilon)
    factor_col = jnp.broadcast_to(factor, (LANES, block)).T
    scaled = (gmid_out_rows[...].astype(f32) * factor_col).astype(bf16)
    down_out[...] += mm(scaled, gained[...], TN)

    @pl.when(place == pl.num_programs(0) - 1)
    def _():
        turn_tiles(grads, 0, down_in[...])
        turn_tiles(grads, out_at, down_out[...])


def adapter_back(meta, gz, grest, normed, mid, gained, gmid, stats, gup_out, up_gate, up_x, up_rest, block, inner_all):
    rows = gz.shape[0]
    inner = gz.shape[1] // 2
    block_rows = lambda width: pl.BlockSpec((block, width), lambda i, *_: (i, 0))
    operands = (gup_out, up_gate, up_x, up_rest)
    columns = 2 * MODEL_WIDTH + REST_LOCAL + 3 * inner
    grid = pltpu.PrefetchScalarGridSpec(
        num_scalar_prefetch=1,
        grid=(rows // block,),
        in_specs=[block_rows(2 * inner), block_rows(REST_LOCAL)]
        + row_specs(block, MODEL_WIDTH, lambda i, meta: i)
        + [block_rows(LANES), block_rows(inner), block_rows(LANES)]
        + [pl.BlockSpec((8, block), lambda i, *_: (0, i))]
        + [whole(a.shape) for a in operands],
        out_specs=[block_rows(LANES), whole((LANES, columns))],
        scratch_shapes=[pltpu.VMEM((LANES, MODEL_WIDTH), f32), pltpu.VMEM((LANES, inner), f32)],
    )
    return pl.pallas_call(
        partial(adapter_back_kernel, inner=inner, inner_all=inner_all),
        out_shape=(
            jax.ShapeDtypeStruct((rows, LANES), bf16),
            jax.ShapeDtypeStruct((LANES, columns), f32),
        ),
        grid_spec=grid,
        compiler_params=params(),
        cost_estimate=pl.CostEstimate(
            flops=2 * rows * LANES * (5 * inner + MODEL_WIDTH), bytes_accessed=20_000_000, transcendentals=0
        ),
    )(meta, gz, grest, *normed, mid, gained, gmid, stats, *operands)


def project_back_kernel(meta, gz, grest, gmid, w_in, down_in, grad_out, *, inner):
    grad = mm(gz[:, 0:inner], w_in[:, inner : 2 * inner], NT)
    grad = grad + mm(gz[:, inner : 2 * inner], w_in[:, 0:inner], NT)
    grad = grad + mm(grest[...], w_in[:, 2 * inner :], NT) + mm(gmid[...], down_in[...], NT)
    grad_out[...] = grad.astype(bf16)


def project_back(meta, gz, grest, gmid, w_in, down_in, half_rows, side):
    inner = gz.shape[1] // 2
    rows_of = lambda width: halves(half_rows, width)[side]
    grid = pltpu.PrefetchScalarGridSpec(
        num_scalar_prefetch=1,
        grid=(MODEL_WIDTH // COLUMNS,),
        in_specs=[
            rows_of(2 * inner), rows_of(REST_LOCAL), rows_of(LANES),
            pl.BlockSpec((COLUMNS, w_in.shape[1]), lambda i, *_: (i, 0)),
            pl.BlockSpec((COLUMNS, LANES), lambda i, *_: (i, 0)),
        ],
        out_specs=pl.BlockSpec((half_rows, COLUMNS), lambda i, *_: (0, i)),
    )
    return pl.pallas_call(
        partial(project_back_kernel, inner=inner),
        out_shape=jax.ShapeDtypeStruct((half_rows, MODEL_WIDTH), bf16),
        grid_spec=grid,
        compiler_params=params(),
        cost_estimate=pl.CostEstimate(
            flops=4 * half_rows * MODEL_WIDTH * inner, bytes_accessed=15_000_000, transcendentals=0
        ),
    )(meta, gz, grest, gmid, w_in, down_in)


def output_kernel(
    meta, key_col, key_row, resid, own, other, stats, cotangent, up_out,
    sent_out, gup_out, *, inner_all,
):
    rows = resid.shape[0]
    row_id = iota((LANES, rows), 0)
    factor = lax.rsqrt(stats[0:1, :] * (1.0 / inner_all) + epsilon)
    factor_col = jnp.where(row_id == 0, factor, 0.0).T[:, 0:1]
    first = meta[META_FIRST]
    summed = (own[...].astype(f32) + other[...].astype(f32)) * factor_col
    mid = (summed[:, MODEL_WIDTH:] * adapter_mask(meta, first, rows)).astype(bf16)
    result = resid[...].astype(f32) + summed[:, 0:MODEL_WIDTH] + mm(mid, up_out[...])
    select = pack_matrix(key_col[...], key_row[...])
    sent_out[...] = mm(select, result.astype(bf16)).astype(bf16)
    gup_out[...] = mm(mid, cotangent[...], TN)


def input_grad_kernel(key_col, key_row, resid, own, other, cotangent, gain, sent_out):
    values = resid[...].astype(f32)
    scale = lax.rsqrt(jnp.mean(values * values, axis=1, keepdims=True) + epsilon)
    weighted = (own[...].astype(f32) + other[...].astype(f32)) * gain[...]
    inner = jnp.mean(weighted * values, axis=1, keepdims=True)
    grad = scale * (weighted - values * (scale * scale * inner))
    result = cotangent[...].astype(f32) + grad
    select = pack_matrix(key_col[...], key_row[...])
    sent_out[...] = mm(select, result.astype(bf16)).astype(bf16)


def finish_kernel(
    key_col, key_row, rows, total, rows_out, gdown_in, gup, gup_rest, gdown_out, gup_out
):
    select = unpack_matrix(key_col[...], key_row[...])
    rows_out[...] = mm(select, rows[...]).astype(bf16)
    inner = gup.shape[2]
    rest_at = 2 * MODEL_WIDTH
    zx_at = rest_at + REST_LOCAL
    out_at = zx_at + 2 * inner
    for first, out in ((0, gdown_in), (out_at, gdown_out)):
        for tile in range(out.shape[0] // LANES):
            span = slice(tile * LANES, (tile + 1) * LANES)
            out[span, :] = total[:, first + tile * LANES : first + (tile + 1) * LANES].astype(f32)
    gup_out[...] = total[:, MODEL_WIDTH:rest_at].astype(f32)
    gup_rest[...] = total[:, rest_at:zx_at].astype(f32)[:, 0 : gup_rest.shape[1]]
    gup[:, 0, :] = total[:, zx_at : zx_at + inner].astype(f32)
    gup[:, 1, :] = total[:, zx_at + inner : out_at].astype(f32)


def body(
    tokens,
    cotangent,
    lengths,
    sequence_adapter,
    perm,
    dealt_position,
    block_norm_gain,
    gate_input_weight,
    rest_weight,
    filter_taps_input,
    filter_taps_bc,
    step_bias,
    head_decay_rate,
    skip_weight,
    gated_norm_gain,
    output_weight,
    adapter_down_in,
    adapter_up_gate_input,
    adapter_up_rest,
    adapter_down_out,
    adapter_up_out,
):
    tensor_count = lax.axis_size("tensor")
    tok_dev = tokens.shape[0]
    group_rows = tok_dev * tensor_count
    heads = step_bias.shape[0]
    inner = heads * HEADDIM
    inner_all = inner * tensor_count
    dp_rank = lax.axis_index("dp")
    tensor_rank = lax.axis_index("tensor")
    dp_count = lax.axis_size("dp")
    swap = [(0, 1), (1, 0)]

    def deal(rows):
        return lax.all_to_all(rows, "dp", split_axis=0, concat_axis=0, tiled=True)

    pairwise = tensor_count == 2
    block = min(BLOCK, group_rows)
    block_count = group_rows // block
    half_count = block_count // 2 if pairwise else block_count

    def gather_rows(mine):
        if pairwise:
            return mine, lax.ppermute(mine, "tensor", swap)
        full = lax.all_gather(mine, "tensor", axis=0, tiled=True)
        return full, full

    def own_rows(full, axis=0):
        return lax.dynamic_slice_in_dim(full, tensor_rank * tok_dev, tok_dev, axis)

    def sum_tensor(values):
        if pairwise:
            return values + lax.ppermute(values, "tensor", swap)
        return lax.psum(values, "tensor")

    def scatter_rows(full):
        summed = lax.psum_scatter(full.astype(f32), "tensor", scatter_dimension=0, tiled=True)
        return summed, jnp.zeros_like(summed)

    bits = [1 << k for k in range(dp_count.bit_length() - 1)]

    def exchange(values, bit):
        pairs = [(k, k ^ bit) for k in range(dp_count)]
        return lax.ppermute(values.astype(bf16), "dp", pairs)

    def sum_dp(values, after):
        height = values.shape[0] // dp_count
        for bit, other_work in zip(bits, [None, *after] + [None] * len(bits)):
            if other_work is not None:
                values, _ = lax.optimization_barrier((values, other_work))
            pairs = values.reshape(values.shape[0] // (2 * height), 2, height, values.shape[1])
            mine = (dp_rank // bit) % 2
            pick = lambda side: lax.dynamic_index_in_dim(pairs, side, 1, keepdims=False).reshape(
                values.shape[0] // 2, values.shape[1]
            )
            values = pick(mine) + exchange(pick(1 - mine), bit).astype(f32)
        return values

    def spread_dp(share):
        return lax.all_gather(share.astype(bf16), "dp", axis=0, tiled=True)

    group_lens = lax.dynamic_slice_in_dim(lengths, dp_rank * SEQ_GROUP, SEQ_GROUP)
    starts = jnp.cumsum(group_lens) - group_lens
    group_ids = lax.dynamic_slice_in_dim(sequence_adapter, dp_rank * SEQ_GROUP, SEQ_GROUP)
    placing = jnp.stack(
        [
            jnp.int32(half_count),
            tensor_rank if pairwise else jnp.int32(0),
            tensor_rank * tok_dev,
            1 - tensor_rank if pairwise else jnp.int32(0),
        ]
    )
    meta = jnp.concatenate([starts, group_ids, placing]).astype(jnp.int32)
    slot = jnp.arange(tok_dev, dtype=jnp.int32)
    given_key = (perm // group_rows) * tok_dev + slot
    dealt_key = (dealt_position // group_rows) * tok_dev + slot

    def keys(values):
        return values[:, None], values[None, :]

    token_rows = jax.ShapeDtypeStruct((tok_dev, MODEL_WIDTH), bf16)
    move_flops = 2 * tok_dev * tok_dev * MODEL_WIDTH
    gain_row = block_norm_gain[None, :]

    dt_start = 2 * STATE + tensor_rank * heads

    def local_rest(matrix):
        steps = lax.dynamic_slice_in_dim(matrix, dt_start, heads, 1)
        return jnp.concatenate(
            [matrix[:, : 2 * STATE], jnp.pad(steps, ((0, 0), (0, LANES - heads)))], axis=1
        )

    def gather_weight(*shards):
        return lax.all_gather(jnp.concatenate(shards, axis=1), "dp", axis=0, tiled=True)

    w_in = gather_weight(
        gate_input_weight[:, 1, :], gate_input_weight[:, 0, :], local_rest(rest_weight)
    )
    w_out = gather_weight(output_weight.T)
    up_rest = local_rest(adapter_up_rest)
    up_gate = adapter_up_gate_input[:, 0, :]
    up_x = adapter_up_gate_input[:, 1, :]
    taps = jnp.pad(filter_taps_input, ((0, 3), (0, 0)))
    taps_bc = jnp.pad(filter_taps_bc, ((0, 3), (0, 0)))
    head_row = lambda values: jnp.pad(values, (0, LANES - heads))[None, :]
    bias_row, decay_row = head_row(step_bias), head_row(head_decay_rate)
    skip_row = jnp.repeat(skip_weight, HEADDIM)[None, :]
    indicator = (
        jnp.arange(inner)[:, None] // HEADDIM == jnp.arange(LANES)[None, :]
    ).astype(bf16)

    sent_tokens, sent_cotangent = simple_call(
        pack_kernel, (token_rows, token_rows), 2 * move_flops, *keys(dealt_position), tokens, cotangent
    )
    resid, normed_mine = simple_call(
        place_norm_kernel, (token_rows, token_rows), move_flops,
        *keys(given_key), deal(sent_tokens), gain_row,
    )
    normed = gather_rows(normed_mine)
    grad_mine = simple_call(
        unpack_kernel, token_rows, move_flops, *keys(given_key), deal(sent_cotangent)
    )
    grad_full = gather_rows(grad_mine)

    gated_gain = gated_norm_gain[None, :]
    x_act, slope, scan_out, gate_pre, gained, states, bc, dbc, dt, sig, mid_in, square = forward_scan(
        meta, normed, w_in, adapter_down_in, up_x, up_rest, up_gate, taps, taps_bc,
        bias_row, decay_row, skip_row, gated_gain, heads, group_rows, block,
    )
    weighted, gmid, stats = out_grad(
        meta, grad_full, gained, square, w_out, adapter_down_out, adapter_up_out, gated_gain, pairwise
    )
    half_rows = tok_dev if pairwise else group_rows
    gained, _ = lax.optimization_barrier((gained, stats))
    part_sent, part_own = out_project(meta, gained, w_out, adapter_down_out, half_rows)
    stats = sum_tensor(stats)
    if pairwise:
        part_sent, stats = lax.optimization_barrier((part_sent, stats))
        part_other = lax.ppermute(part_sent, "tensor", swap)
    else:
        part_own, part_other = scatter_rows(part_sent)

    gz, grest = backward_scan(
        meta, scan_out, gate_pre, weighted, x_act, slope, bc, dbc, dt, sig, states, stats,
        taps, taps_bc, decay_row, skip_row, indicator, heads, inner_all,
    )
    part_other, _ = lax.optimization_barrier((part_other, gz))
    sent_output, gup_out = simple_call(
        partial(output_kernel, inner_all=inner_all),
        (token_rows, jax.ShapeDtypeStruct((LANES, MODEL_WIDTH), f32)), 2 * move_flops,
        meta, *keys(perm), resid, part_own, part_other,
        own_rows(stats, 1), grad_mine, adapter_up_out, scalars=1,
    )
    dealt_output = deal(sent_output)
    gmid_in, gradients = adapter_back(
        meta, gz, grest, normed, mid_in, gained, gmid, stats, gup_out, up_gate, up_x, up_rest,
        block, inner_all,
    )
    gz, _ = lax.optimization_barrier((gz, gradients))
    back = partial(project_back, meta, gz, grest, gmid_in, w_in, adapter_down_in, half_rows)
    if pairwise:
        sent_back = back(0)
        grad_other = lax.ppermute(sent_back, "tensor", swap)
        gz, _, dealt_output = lax.optimization_barrier((gz, sent_back, dealt_output))
        grad_own = project_back(meta, gz, grest, gmid_in, w_in, adapter_down_in, half_rows, 1)
    else:
        grad_own, grad_other = scatter_rows(back(0))
    output = simple_call(unpack_kernel, token_rows, move_flops, *keys(dealt_key), dealt_output)
    grad_other, output = lax.optimization_barrier((grad_other, output))
    sent_grad = simple_call(
        input_grad_kernel, token_rows, move_flops,
        *keys(perm), resid, grad_own, grad_other, grad_mine, gain_row,
    )

    rest_at = 2 * MODEL_WIDTH
    zx_at = rest_at + REST_LOCAL
    out_at = zx_at + 2 * inner
    total = sum_dp(gradients, (sent_back, grad_own, grad_other) if pairwise else ())
    steps = total[:, rest_at + 2 * STATE : rest_at + 2 * STATE + heads]
    wide = jnp.zeros((total.shape[0], LANES), f32)
    wide = lax.dynamic_update_slice(wide, steps, (0, tensor_rank * heads))
    shared = jnp.concatenate([total[:, : rest_at + 2 * STATE], wide], axis=1)
    share = jnp.concatenate([sum_tensor(shared), total[:, zx_at:]], axis=1)
    share, sent_grad = lax.optimization_barrier((share, sent_grad))
    total = spread_dp(share)
    dealt_grad = deal(sent_grad)
    input_grad, gdown_in, gup_zx, gup_rest, gdown_out, gup_out = simple_call(
        finish_kernel,
        (
            token_rows,
            jax.ShapeDtypeStruct((MODEL_WIDTH, LANES), f32),
            jax.ShapeDtypeStruct((LANES, 2, inner), f32),
            jax.ShapeDtypeStruct((LANES, adapter_up_rest.shape[1]), f32),
            jax.ShapeDtypeStruct((inner, LANES), f32),
            jax.ShapeDtypeStruct((LANES, MODEL_WIDTH), f32),
        ),
        move_flops, *keys(dealt_key), dealt_grad, total,
    )
    return output, input_grad, gdown_in, gup_zx, gup_rest, gdown_out, gup_out


def solution(mesh):
    placed = (
        P(("dp", "tensor"), None),
        P(("dp", "tensor"), None),
        P(),
        P(),
        P(("dp", "tensor")),
        P(("dp", "tensor")),
        P(),
        P("dp", None, "tensor"),
        P("dp", None),
        P(None, "tensor"),
        P(),
        P("tensor"),
        P("tensor"),
        P("tensor"),
        P("tensor"),
        P("tensor", "dp"),
        P(),
        P(None, None, "tensor"),
        P(),
        P("tensor", None),
        P(),
    )
    return jax.shard_map(
        body,
        mesh=mesh,
        in_specs=placed,
        out_specs=(
            P(("dp", "tensor"), None),
            P(("dp", "tensor"), None),
            P(),
            P(None, None, "tensor"),
            P(),
            P("tensor", None),
            P(),
        ),
        check_vma=False,
    )
```

```python
from functools import partial

import jax
import jax.numpy as jnp
import numpy as np
from jax import lax
from jax.experimental import pallas as pl
from jax.experimental.pallas import tpu as pltpu
from jax.sharding import PartitionSpec as P

MODEL_WIDTH = 1536
HEADDIM = 64
STATE = 128
LANES = 128
CHUNK = 128
BLOCK = 256
ADAPTER_RANK = 16
SEQ_GROUP = 4
REST_LOCAL = 2 * STATE + LANES
META_HALF = 2 * SEQ_GROUP
META_RANK = META_HALF + 1
META_FIRST = META_HALF + 2
META_THEIRS = META_HALF + 3
COLUMNS = 512

epsilon = 1e-05
LOG2E = 1.4426950408889634
VMEM_BYTES = 56 * 1024 * 1024
f32 = jnp.float32
bf16 = jnp.bfloat16

NN = (((1,), (0,)), ((), ()))
NT = (((1,), (1,)), ((), ()))
TN = (((0,), (0,)), ((), ()))


def mm(left, right, dims=NN):
    return lax.dot_general(left, right, dims, preferred_element_type=f32)


def params(count=1):
    return pltpu.CompilerParams(
        dimension_semantics=("arbitrary",) * count, vmem_limit_bytes=VMEM_BYTES
    )


def whole(shape):
    return pl.BlockSpec(shape, lambda *_: (0,) * len(shape))


def iota(shape, axis):
    return lax.broadcasted_iota(jnp.int32, shape, axis)


def pack_matrix(key_col, key_row):
    count = key_row.shape[1]
    rank = jnp.sum((key_col < key_row).astype(f32), axis=0, keepdims=True).astype(jnp.int32)
    return (iota((count, count), 0) == rank).astype(f32).astype(bf16)


def unpack_matrix(key_col, key_row):
    count = key_row.shape[1]
    rank = jnp.sum((key_row < key_col).astype(f32), axis=1, keepdims=True).astype(jnp.int32)
    return (iota((count, count), 1) == rank).astype(f32).astype(bf16)


def pack_kernel(key_col, key_row, first, second, first_out, second_out):
    select = pack_matrix(key_col[...], key_row[...])
    first_out[...] = mm(select, first[...]).astype(bf16)
    second_out[...] = mm(select, second[...]).astype(bf16)


def unpack_kernel(key_col, key_row, rows, rows_out):
    select = unpack_matrix(key_col[...], key_row[...])
    rows_out[...] = mm(select, rows[...]).astype(bf16)


def place_norm_kernel(key_col, key_row, rows, gain, rows_out, normed_out):
    select = unpack_matrix(key_col[...], key_row[...])
    resid = mm(select, rows[...])
    rows_out[...] = resid.astype(bf16)
    scale = lax.rsqrt(jnp.mean(resid * resid, axis=1, keepdims=True) + epsilon)
    normed_out[...] = (resid * scale * gain[...]).astype(bf16)


def simple_call(kernel, outs, flops, *args, scalars=0):
    vector = pl.BlockSpec(memory_space=pltpu.VMEM)
    scalar = pl.BlockSpec(memory_space=pltpu.SMEM)
    return pl.pallas_call(
        kernel,
        out_shape=outs,
        in_specs=[scalar] * scalars + [vector] * (len(args) - scalars),
        out_specs=jax.tree.map(lambda _: vector, outs),
        compiler_params=pltpu.CompilerParams(vmem_limit_bytes=VMEM_BYTES),
        cost_estimate=pl.CostEstimate(flops=flops, bytes_accessed=1_000_000, transcendentals=0),
    )(*args)


def segment_start(meta, position):
    begin = jnp.zeros_like(position)
    for k in range(1, SEQ_GROUP):
        begin = jnp.where(position >= meta[k], meta[k], begin)
    return begin


def row_specs(block, width, place, scale=1):
    def spec(side):
        def index(i, meta):
            half = meta[META_HALF] * scale
            return (jnp.clip(place(i, meta) - meta[side] * half, 0, half - 1), 0)

        return pl.BlockSpec((block, width), index)

    return [spec(META_RANK), spec(META_THEIRS)]


def pick_rows(meta, place, mine, other, scale=1):
    own = place // (meta[META_HALF] * scale) == meta[META_RANK]
    return jnp.where(own, mine[...], other[...])


def adapter_mask(meta, first, rows):
    position = first + iota((rows, LANES), 0)
    owner = jnp.full((rows, LANES), meta[SEQ_GROUP], jnp.int32)
    for k in range(1, SEQ_GROUP):
        owner = jnp.where(position >= meta[k], meta[SEQ_GROUP + k], owner)
    return (iota((rows, LANES), 1) // ADAPTER_RANK == owner).astype(f32)


def cumulate(values):
    total = values
    step = 1
    while step < values.shape[0]:
        pad = jnp.zeros((step, values.shape[1]), f32)
        total = total + jnp.concatenate([pad, total[:-step]], axis=0)
        step *= 2
    return total


def cumulate_back(values):
    total = values
    step = 1
    while step < values.shape[0]:
        pad = jnp.zeros((step, values.shape[1]), f32)
        total = total + jnp.concatenate([total[step:], pad], axis=0)
        step *= 2
    return total


def sigmoid(values):
    return 0.5 * jnp.tanh(0.5 * values) + 0.5


def column(values, h):
    return jnp.broadcast_to(values[:, h : h + 1], (values.shape[0], LANES))


def decay_tables(dt, decay_rate):
    cumul = cumulate(dt * (-LOG2E * decay_rate))
    source = cumul - jnp.log(jnp.maximum(dt, 1e-37)) * LOG2E
    return cumul, source


def forward_kernel(
    meta,
    mine, other, w_in, down_in, up_x, up_rest, up_gate, taps, taps_bc, step_bias, decay_rate, skip, gain,
    x_out, dx_out, y_out, gate_out, gained_out, state_out, bc_out, dbc_out, dt_out, sig_out, mid_out,
    square_out,
    conv_in, rest, gate_pre, state, from_state, scaled,
    *, heads, block,
):
    i = pl.program_id(0)
    inner = heads * HEADDIM
    per_block = block // CHUNK
    first = i * CHUNK

    @pl.when(i == 0)
    def _():
        conv_in[block : block + 8, :] = jnp.zeros((8, inner), f32)
        rest[block : block + 8, :] = jnp.zeros((8, REST_LOCAL), f32)
        state[...] = jnp.zeros_like(state)

    @pl.when(i % per_block == 0)
    def _():
        conv_in[0:8, :] = conv_in[block : block + 8, :]
        rest[0:8, :] = rest[block : block + 8, :]
        rows = pick_rows(meta, i // per_block, mine, other)
        mid = (mm(rows, down_in[...]) * adapter_mask(meta, first, block)).astype(bf16)
        mid_out[...] = mid
        conv_in[8 : block + 8, :] = mm(rows, w_in[:, 0:inner]) + mm(mid, up_x[...])
        gate_pre[...] = mm(rows, w_in[:, inner : 2 * inner]) + mm(mid, up_gate[...])
        rest[8 : block + 8, :] = mm(rows, w_in[:, 2 * inner :]) + mm(mid, up_rest[...])

    offset = pl.multiple_of((i % per_block) * CHUNK, CHUNK)
    window = pl.ds(offset, CHUNK + 8)
    position = first + iota((CHUNK, LANES), 0)
    begin = segment_start(meta, position)
    depth = position - begin
    same = [(depth >= k).astype(f32) for k in (1, 2, 3)]

    def conv(ext, tap):
        summed = tap[3:4] * ext[8:] + tap[4:5]
        for k in (1, 2, 3):
            summed = summed + tap[3 - k : 4 - k] * (ext[8 - k : 8 - k + CHUNK] * same[k - 1])
        sig = sigmoid(summed)
        act = summed * sig
        return act, sig + act * (1.0 - sig)

    b_act, b_slope = conv(rest[window, 0:STATE], taps_bc[:, 0:STATE])
    c_act, c_slope = conv(rest[window, STATE : 2 * STATE], taps_bc[:, STATE : 2 * STATE])
    b_mat = b_act.astype(bf16)
    c_mat = c_act.astype(bf16)
    bc_out[:, 0:STATE] = b_mat
    bc_out[:, STATE : 2 * STATE] = c_mat
    dbc_out[:, 0:STATE] = b_slope
    dbc_out[:, STATE : 2 * STATE] = c_slope
    step_pre = rest[window, 2 * STATE : REST_LOCAL][8:] + step_bias[...]
    dt = jnp.maximum(step_pre, 0.0) + jnp.log(1.0 + jnp.exp(-jnp.abs(step_pre)))
    small = jnp.exp(step_pre)
    dt = jnp.where(step_pre < -8.0, small * (1.0 - 0.5 * small), dt)
    dt_out[...] = dt
    sig_out[...] = sigmoid(step_pre)
    cumul, source = decay_tables(dt, decay_rate[...])
    source_rows = source.T
    total = cumul[CHUNK - 1 : CHUNK, :]
    s_pos = first + iota((CHUNK, CHUNK), 1)
    allowed = jnp.where((s_pos <= position) & (s_pos >= begin), 0.0, -1e30)
    scores = mm(c_mat, b_mat, NT)
    begin_last = segment_start(meta, first + CHUNK - 1)
    kept = jnp.where(begin_last < first, 1.0, 0.0)
    in_last = (position >= begin_last).astype(f32)
    carried = (begin < first).astype(f32)
    state_low = state[...].astype(bf16)
    state_out[...] = state_low
    from_state[...] = mm(c_mat, state_low)
    left = iota((CHUNK, LANES), 1) < HEADDIM
    left_row = left[0:1]
    square = jnp.zeros((CHUNK, LANES), f32)
    for pair in range(heads // 2):
        h0, h1 = 2 * pair, 2 * pair + 1
        cols = slice(pair * LANES, (pair + 1) * LANES)
        act, slope = conv(conv_in[window, cols], taps[:, cols])
        x_low = act.astype(bf16)
        x_out[:, cols] = x_low
        dx_out[:, cols] = slope.astype(bf16)
        x = x_low.astype(f32)
        cum0, cum1 = column(cumul, h0), column(cumul, h1)
        m0 = jnp.exp2(cum0 - source_rows[h0 : h0 + 1] + allowed) * scores
        m1 = jnp.exp2(cum1 - source_rows[h1 : h1 + 1] + allowed) * scores
        weights = jnp.concatenate([m0.astype(bf16), m1.astype(bf16)], axis=1)
        x_split = jnp.concatenate(
            [jnp.where(left, x, 0.0).astype(bf16), jnp.where(left, 0.0, x).astype(bf16)], axis=0
        )
        inside = mm(weights, x_split)
        reach = jnp.exp2(jnp.where(left, cum0, cum1)) * carried
        y = inside + reach * from_state[:, cols] + skip[:, cols] * x
        y_out[:, cols] = y
        gate = gate_pre[pl.ds(offset, CHUNK), cols]
        gate_out[:, cols] = gate
        gated = y * (gate * sigmoid(gate))
        square = square + gated * gated
        gained_out[:, cols] = (gated * gain[:, cols]).astype(bf16)
        total_pair = jnp.where(left_row, column(total, h0), column(total, h1))
        source_pair = jnp.where(left, column(source, h0), column(source, h1))
        coefficient = jnp.exp2(total_pair - source_pair) * in_last
        scaled[:, cols] = (x * coefficient).astype(bf16)
        state[:, cols] = state[:, cols] * (jnp.exp2(total_pair) * kept)
    state[...] += mm(b_mat, scaled[...], TN)
    square_out[...] = jnp.sum(square.T, axis=0, keepdims=True)


def forward_scan(meta, normed, w_in, down_in, up_x, up_rest, up_gate, taps, taps_bc, bias, decay, skip, gain, heads, rows, block):
    inner = heads * HEADDIM
    per_block = block // CHUNK
    chunk_rows = lambda width: pl.BlockSpec((CHUNK, width), lambda i, *_: (i, 0))
    block_rows = lambda width: pl.BlockSpec((block, width), lambda i, *_: (i // per_block, 0))
    outs = (
        jax.ShapeDtypeStruct((rows, inner), bf16),
        jax.ShapeDtypeStruct((rows, inner), bf16),
        jax.ShapeDtypeStruct((rows, inner), f32),
        jax.ShapeDtypeStruct((rows, inner), f32),
        jax.ShapeDtypeStruct((rows, inner), bf16),
        jax.ShapeDtypeStruct((rows // CHUNK * STATE, inner), bf16),
        jax.ShapeDtypeStruct((rows, 2 * STATE), bf16),
        jax.ShapeDtypeStruct((rows, 2 * STATE), f32),
        jax.ShapeDtypeStruct((rows, LANES), f32),
        jax.ShapeDtypeStruct((rows, LANES), f32),
        jax.ShapeDtypeStruct((rows, LANES), bf16),
        jax.ShapeDtypeStruct((1, rows), f32),
    )
    operands = (w_in, down_in, up_x, up_rest, up_gate, taps, taps_bc, bias, decay, skip, gain)
    grid = pltpu.PrefetchScalarGridSpec(
        num_scalar_prefetch=1,
        grid=(rows // CHUNK,),
        in_specs=row_specs(block, MODEL_WIDTH, lambda i, meta: i // per_block)
        + [whole(a.shape) for a in operands],
        out_specs=[
            chunk_rows(inner), chunk_rows(inner), chunk_rows(inner), chunk_rows(inner),
            chunk_rows(inner), chunk_rows(inner),
            chunk_rows(2 * STATE), chunk_rows(2 * STATE), chunk_rows(LANES), chunk_rows(LANES),
            block_rows(LANES), pl.BlockSpec((1, CHUNK), lambda i, *_: (0, i)),
        ],
        scratch_shapes=[
            pltpu.VMEM((block + 8, inner), f32),
            pltpu.VMEM((block + 8, REST_LOCAL), f32),
            pltpu.VMEM((block, inner), f32),
            pltpu.VMEM((STATE, inner), f32),
            pltpu.VMEM((CHUNK, inner), f32),
            pltpu.VMEM((CHUNK, inner), bf16),
        ],
    )
    return pl.pallas_call(
        partial(forward_kernel, heads=heads, block=block),
        out_shape=outs,
        grid_spec=grid,
        compiler_params=params(),
        cost_estimate=pl.CostEstimate(
            flops=5 * rows * MODEL_WIDTH * inner, bytes_accessed=50_000_000, transcendentals=0
        ),
    )(meta, *normed, *operands)


def out_grad_kernel(
    meta,
    gd_mine, gd_other, gained, square, w_out, down_out, up_out, gain,
    weighted_out, gmid_out, stats_out,
    gd, cross,
    *, pairwise,
):
    step = pl.program_id(0)
    rows = gd.shape[0]

    @pl.when(step == 0)
    def _():
        if pairwise:
            tokens = gd_mine.shape[0]
            gd[pl.ds(pl.multiple_of(meta[META_FIRST], LANES), tokens), :] = gd_mine[...]
            gd[pl.ds(pl.multiple_of(rows - tokens - meta[META_FIRST], LANES), tokens), :] = gd_other[...]
        else:
            gd[...] = gd_mine[...]
        gmid = mm(gd[...], up_out[...], NT) * adapter_mask(meta, 0, rows)
        gmid_out[...] = gmid.astype(bf16)
        cross[...] = jnp.zeros_like(cross)

    grad = mm(gd[...], w_out[...]) + mm(gmid_out[...], down_out[...], NT)
    weighted_out[...] = grad * gain[...]
    product = grad * gained[...].astype(f32)
    total = cross[...]
    for tile in range(product.shape[1] // LANES):
        total = total + product[:, tile * LANES : (tile + 1) * LANES]
    cross[...] = total

    @pl.when(step == pl.num_programs(0) - 1)
    def _():
        row = jnp.sum(cross[...].T, axis=0, keepdims=True)
        stats_out[...] = jnp.where(iota((8, rows), 0) == 0, square[...], row)


def out_grad(meta, cotangent, gained, square, w_out, down_out, up_out, gain, pairwise):
    rows, inner = gained.shape
    width = 4 * LANES if inner % (4 * LANES) == 0 else LANES
    columns = lambda height: pl.BlockSpec((height, width), lambda i, *_: (0, i))
    outs = (
        jax.ShapeDtypeStruct((rows, inner), f32),
        jax.ShapeDtypeStruct((rows, LANES), bf16),
        jax.ShapeDtypeStruct((8, rows), f32),
    )
    grid = pltpu.PrefetchScalarGridSpec(
        num_scalar_prefetch=1,
        grid=(inner // width,),
        in_specs=[
            whole(cotangent[0].shape), whole(cotangent[1].shape), columns(rows), whole(square.shape),
            columns(MODEL_WIDTH), pl.BlockSpec((width, LANES), lambda i, *_: (i, 0)),
            whole(up_out.shape), columns(1),
        ],
        out_specs=[columns(rows), whole(outs[1].shape), whole(outs[2].shape)],
        scratch_shapes=[pltpu.VMEM((rows, MODEL_WIDTH), bf16), pltpu.VMEM((rows, LANES), f32)],
    )
    return pl.pallas_call(
        partial(out_grad_kernel, pairwise=pairwise),
        out_shape=outs,
        grid_spec=grid,
        compiler_params=params(),
        cost_estimate=pl.CostEstimate(
            flops=2 * rows * MODEL_WIDTH * inner, bytes_accessed=20_000_000, transcendentals=0
        ),
    )(meta, *cotangent, gained, square, w_out, down_out, up_out, gain)


def halves(meta_rows, width):
    theirs = pl.BlockSpec((meta_rows, width), lambda i, meta: (meta[META_THEIRS], 0))
    own = pl.BlockSpec((meta_rows, width), lambda i, meta: (meta[META_RANK], 0))
    return theirs, own


def out_project_kernel(meta, theirs, own, w_out, down_out, sent_out, kept_out):
    step = pl.program_id(0)
    width = w_out.shape[0]
    columns = pl.ds(pl.multiple_of(step * width, LANES), width)
    sent_out[:, columns] = mm(theirs[...], w_out[...], NT).astype(bf16)
    kept_out[:, columns] = mm(own[...], w_out[...], NT).astype(bf16)

    @pl.when(step == 0)
    def _():
        sent_out[:, MODEL_WIDTH:] = mm(theirs[...], down_out[...]).astype(bf16)
        kept_out[:, MODEL_WIDTH:] = mm(own[...], down_out[...]).astype(bf16)


def out_project(meta, gained, w_out, down_out, half_rows):
    inner = gained.shape[1]
    out = jax.ShapeDtypeStruct((half_rows, MODEL_WIDTH + LANES), bf16)
    grid = pltpu.PrefetchScalarGridSpec(
        num_scalar_prefetch=1,
        grid=(MODEL_WIDTH // COLUMNS,),
        in_specs=[
            *halves(half_rows, inner),
            pl.BlockSpec((COLUMNS, inner), lambda i, *_: (i, 0)),
            whole(down_out.shape),
        ],
        out_specs=[whole(out.shape)] * 2,
    )
    return pl.pallas_call(
        out_project_kernel,
        out_shape=(out, out),
        grid_spec=grid,
        compiler_params=params(),
        cost_estimate=pl.CostEstimate(
            flops=4 * half_rows * MODEL_WIDTH * inner, bytes_accessed=15_000_000, transcendentals=0
        ),
    )(meta, gained, gained, w_out, down_out)


def split_sum(values, indicator):
    high = values.astype(bf16)
    low = (values - high.astype(f32)).astype(bf16)
    return mm(high, indicator) + mm(low, indicator)


def turn_tiles(out, first, values):
    for tile in range(values.shape[1] // LANES):
        out[:, first + tile * LANES : first + (tile + 1) * LANES] = values[
            :, tile * LANES : (tile + 1) * LANES
        ].T


def backward_kernel(
    meta,
    scan_out, gate_pre, weighted, x_in, slope_in, bc_in, dbc_in, dt_in, sig_in, state_in, stats,
    normed_mine, normed_other, mid_rows, gained, gmid_rows,
    taps, taps_bc, decay_rate, skip, indicator, up_gate, up_x, up_rest,
    gz_out, grest_out, gmid_out, grads,
    down_in, down_out, dstate, g_next, gbc_next, from_dstate, scaled, reached, product, source_product,
    *, heads, inner_all, scale,
):
    i = pl.program_id(0)
    inner = heads * HEADDIM
    place = pl.num_programs(0) - 1 - i
    first = place * CHUNK
    rest_at = 2 * MODEL_WIDTH
    zx_at = rest_at + REST_LOCAL
    out_at = zx_at + 2 * inner

    @pl.when(i == 0)
    def _():
        dstate[...] = jnp.zeros_like(dstate)
        g_next[...] = jnp.zeros_like(g_next)
        gbc_next[...] = jnp.zeros_like(gbc_next)
        product[CHUNK:, :] = jnp.zeros((8, inner), f32)
        grads[...] = jnp.zeros_like(grads)
        down_in[...] = jnp.zeros_like(down_in)
        down_out[...] = jnp.zeros_like(down_out)

    s_pos = first + iota((CHUNK, LANES), 0)
    begin = segment_start(meta, s_pos)
    long_pos = first + iota((CHUNK + 8, LANES), 0)
    long_depth = long_pos - segment_start(meta, long_pos)
    same = [(long_depth >= k).astype(f32) for k in (1, 2, 3)]
    t_pos = first + iota((CHUNK, CHUNK), 1)
    t_begin = segment_start(meta, t_pos)
    allowed = jnp.where((s_pos <= t_pos) & (s_pos >= t_begin), 0.0, -1e30)
    begin_last = segment_start(meta, first + CHUNK - 1)
    kept = jnp.where(begin_last < first, 1.0, 0.0)
    in_last = (s_pos >= begin_last).astype(f32)
    carried = (begin < first).astype(f32)

    factor = lax.rsqrt(stats[0:1, :] * (1.0 / inner_all) + epsilon)
    pull = factor * factor * factor * stats[1:2, :] * (1.0 / inner_all)
    row_id = iota((LANES, CHUNK), 0)
    both = jnp.where(row_id == 0, factor, jnp.where(row_id == 1, pull, 0.0)).T
    factor_col, pull_col = column(both, 0), column(both, 1)
    gmid_scaled = (gmid_rows[...].astype(f32) * factor_col).astype(bf16)
    down_out[...] += mm(gmid_scaled, gained[...], TN)
    mid_turned = mid_rows[...].astype(f32).T.astype(bf16)

    dt = dt_in[...]
    sig = sig_in[...]
    cumul, source = decay_tables(dt, decay_rate[...])
    cumul_rows = cumul.T
    total = cumul[CHUNK - 1 : CHUNK, :]
    b_mat = bc_in[:, 0:STATE]
    c_mat = bc_in[:, STATE : 2 * STATE]
    scores = mm(b_mat, c_mat, NT)
    dstate_low = dstate[...].astype(bf16)
    from_dstate[...] = mm(b_mat, dstate_low)
    left = iota((CHUNK, LANES), 1) < HEADDIM
    left_row = left[0:1]
    gscores = jnp.zeros((CHUNK, CHUNK), f32)

    def conv_back(grad, later, tap):
        ext = jnp.concatenate([grad, later], axis=0)
        out = tap[3:4] * grad
        for k in (1, 2, 3):
            out = out + tap[3 - k : 4 - k] * (ext * same[k - 1])[k : k + CHUNK]
        return out

    for pair in range(heads // 2):
        h0, h1 = 2 * pair, 2 * pair + 1
        cols = slice(pair * LANES, (pair + 1) * LANES)
        gate = gate_pre[:, cols]
        y = scan_out[:, cols]
        gate_sig = sigmoid(gate)
        silu = gate * gate_sig
        ggated = weighted[:, cols] * factor_col - y * silu * pull_col
        gy_low = (ggated * silu).astype(bf16)
        ggate = (ggated * y * (gate_sig + silu * (1.0 - gate_sig))).astype(bf16)
        gz_out[:, cols] = ggate
        gy = gy_low.astype(f32)
        gy_split = jnp.concatenate(
            [jnp.where(left, gy, 0.0).astype(bf16), jnp.where(left, 0.0, gy).astype(bf16)], axis=0
        )
        x_low = x_in[:, cols]
        x = x_low.astype(f32)
        dots = mm(x_low, gy_split, NT)
        src0, src1 = column(source, h0), column(source, h1)
        e0 = jnp.exp2(cumul_rows[h0 : h0 + 1] - src0 + allowed)
        e1 = jnp.exp2(cumul_rows[h1 : h1 + 1] - src1 + allowed)
        gscores = gscores + dots[:, 0:CHUNK] * e0 + dots[:, CHUNK:] * e1
        weights = jnp.concatenate([(e0 * scores).astype(bf16), (e1 * scores).astype(bf16)], axis=1)
        inside = mm(weights, gy_split)
        total_pair = jnp.where(left_row, column(total, h0), column(total, h1))
        coefficient = jnp.exp2(total_pair - jnp.where(left, src0, src1)) * in_last
        reach = jnp.exp2(jnp.where(left, column(cumul, h0), column(cumul, h1))) * carried
        outside = coefficient * from_dstate[:, cols]
        gx_scan = inside + outside
        skip_row = skip[:, cols]
        gx = gx_scan + skip_row * gy
        x_side = x * gx_scan
        source_product[:, cols] = x_side.astype(bf16)
        product[0:CHUNK, cols] = gy * (y - skip_row * x) - x_side
        scaled[:, cols] = (x * coefficient).astype(bf16)
        reached[:, cols] = (gy * reach).astype(bf16)
        keep_row = jnp.exp2(total_pair) * kept
        dstate_cols = dstate[:, cols]
        product[CHUNK : CHUNK + 1, cols] = jnp.sum(x * outside, axis=0, keepdims=True) + keep_row * jnp.sum(
            dstate_cols * state_in[:, cols].astype(f32), axis=0, keepdims=True
        )
        dstate[:, cols] = dstate_cols * keep_row
        gconv = gx * slope_in[:, cols].astype(f32)
        later = slice(inner + pair * LANES, inner + (pair + 1) * LANES)
        gconv_in = conv_back(gconv, g_next[:, cols], taps[:, cols]).astype(bf16)
        gz_out[:, later] = gconv_in
        g_next[:, cols] = gconv[0:8]

    gscores_low = gscores.astype(bf16)
    grad_b = mm(gscores_low, c_mat) + mm(scaled[...], dstate_low, NT)
    grad_c = mm(gscores_low, b_mat, TN) + mm(reached[...], state_in[...], NT)
    for part, grad in ((0, grad_b), (1, grad_c)):
        cols = slice(part * STATE, (part + 1) * STATE)
        gconv = grad * dbc_in[:, cols]
        grest_out[:, cols] = conv_back(gconv, gbc_next[:, cols], taps_bc[:, cols]).astype(bf16)
        gbc_next[:, cols] = gconv[0:8]
    dstate[...] += mm(c_mat, reached[...], TN)

    sums = split_sum(product[...], indicator[...])
    direct = mm(source_product[...], indicator[...])
    grad_log = cumulate_back(sums[0:CHUNK]) + sums[CHUNK : CHUNK + 1]
    ratio = jnp.where(dt > 1e-30, sig / jnp.maximum(dt, 1e-30), 1.0)
    grad_pre = direct * ratio - decay_rate[...] * grad_log * sig
    used = iota((CHUNK, LANES), 1) < heads
    grest_out[:, 2 * STATE : REST_LOCAL] = jnp.where(used, grad_pre, 0.0).astype(bf16)

    grest = grest_out[...]
    gmid = mm(gz_out[:, 0:inner], up_gate[...], NT) + mm(gz_out[:, inner:], up_x[...], NT)
    gmid = gmid + mm(grest, up_rest[...], NT)
    grads[:, zx_at:out_at] += mm(mid_turned, gz_out[...])
    gmid = (gmid * adapter_mask(meta, first, CHUNK)).astype(bf16)
    gmid_out[...] = gmid
    grads[:, rest_at:zx_at] += mm(mid_turned, grest)
    down_in[...] += mm(gmid, pick_rows(meta, place, normed_mine, normed_other, scale), TN)

    @pl.when(place == 0)
    def _():
        turn_tiles(grads, 0, down_in[...])
        turn_tiles(grads, out_at, down_out[...])


def backward_scan(meta, scan_out, gate_pre, weighted, x_act, slope, bc, dbc, dt, sig, states, stats, normed, mid, gained, gmid, taps, taps_bc, decay, skip, indicator, up_gate, up_x, up_rest, heads, inner_all, block):
    rows, inner = scan_out.shape
    count = rows // CHUNK
    chunk_rows = lambda width: pl.BlockSpec((CHUNK, width), lambda i, *_: (count - 1 - i, 0))
    scale = block // CHUNK
    columns = 2 * MODEL_WIDTH + REST_LOCAL + 3 * inner
    operands = (taps, taps_bc, decay, skip, indicator, up_gate, up_x, up_rest)
    streams = (scan_out, gate_pre, weighted, x_act, slope, bc, dbc, dt, sig, states)
    outs = (
        jax.ShapeDtypeStruct((rows, 2 * inner), bf16),
        jax.ShapeDtypeStruct((rows, REST_LOCAL), bf16),
        jax.ShapeDtypeStruct((rows, LANES), bf16),
        jax.ShapeDtypeStruct((LANES, columns), f32),
    )
    grid = pltpu.PrefetchScalarGridSpec(
        num_scalar_prefetch=1,
        grid=(count,),
        in_specs=[chunk_rows(a.shape[1]) for a in streams]
        + [pl.BlockSpec((8, CHUNK), lambda i, *_: (0, count - 1 - i))]
        + row_specs(CHUNK, MODEL_WIDTH, lambda i, meta: count - 1 - i, scale)
        + [chunk_rows(LANES), chunk_rows(inner), chunk_rows(LANES)]
        + [whole(a.shape) for a in operands],
        out_specs=[
            chunk_rows(2 * inner), chunk_rows(REST_LOCAL), chunk_rows(LANES), whole((LANES, columns))
        ],
        scratch_shapes=[
            pltpu.VMEM((LANES, MODEL_WIDTH), f32),
            pltpu.VMEM((LANES, inner), f32),
            pltpu.VMEM((STATE, inner), f32),
            pltpu.VMEM((8, inner), f32),
            pltpu.VMEM((8, 2 * STATE), f32),
            pltpu.VMEM((CHUNK, inner), f32),
            pltpu.VMEM((CHUNK, inner), bf16),
            pltpu.VMEM((CHUNK, inner), bf16),
            pltpu.VMEM((CHUNK + 8, inner), f32),
            pltpu.VMEM((CHUNK, inner), bf16),
        ],
    )
    return pl.pallas_call(
        partial(backward_kernel, heads=heads, inner_all=inner_all, scale=scale),
        out_shape=outs,
        grid_spec=grid,
        compiler_params=params(),
        cost_estimate=pl.CostEstimate(
            flops=6 * rows * MODEL_WIDTH * inner, bytes_accessed=50_000_000, transcendentals=0
        ),
    )(meta, *streams, stats, *normed, mid, gained, gmid, *operands)


def project_back_kernel(meta, gz, grest, gmid, w_in, down_in, grad_out, *, inner):
    grad = mm(gz[:, 0:inner], w_in[:, inner : 2 * inner], NT)
    grad = grad + mm(gz[:, inner : 2 * inner], w_in[:, 0:inner], NT)
    grad = grad + mm(grest[...], w_in[:, 2 * inner :], NT) + mm(gmid[...], down_in[...], NT)
    grad_out[...] = grad.astype(bf16)


def project_back(meta, gz, grest, gmid, w_in, down_in, half_rows, side):
    inner = gz.shape[1] // 2
    rows_of = lambda width: halves(half_rows, width)[side]
    grid = pltpu.PrefetchScalarGridSpec(
        num_scalar_prefetch=1,
        grid=(MODEL_WIDTH // COLUMNS,),
        in_specs=[
            rows_of(2 * inner), rows_of(REST_LOCAL), rows_of(LANES),
            pl.BlockSpec((COLUMNS, w_in.shape[1]), lambda i, *_: (i, 0)),
            pl.BlockSpec((COLUMNS, LANES), lambda i, *_: (i, 0)),
        ],
        out_specs=pl.BlockSpec((half_rows, COLUMNS), lambda i, *_: (0, i)),
    )
    return pl.pallas_call(
        partial(project_back_kernel, inner=inner),
        out_shape=jax.ShapeDtypeStruct((half_rows, MODEL_WIDTH), bf16),
        grid_spec=grid,
        compiler_params=params(),
        cost_estimate=pl.CostEstimate(
            flops=4 * half_rows * MODEL_WIDTH * inner, bytes_accessed=15_000_000, transcendentals=0
        ),
    )(meta, gz, grest, gmid, w_in, down_in)


def output_kernel(
    meta, key_col, key_row, resid, own, other, stats, cotangent, up_out,
    sent_out, gup_out, *, inner_all,
):
    rows = resid.shape[0]
    row_id = iota((LANES, rows), 0)
    factor = lax.rsqrt(stats[0:1, :] * (1.0 / inner_all) + epsilon)
    factor_col = jnp.where(row_id == 0, factor, 0.0).T[:, 0:1]
    first = meta[META_FIRST]
    summed = (own[...].astype(f32) + other[...].astype(f32)) * factor_col
    mid = (summed[:, MODEL_WIDTH:] * adapter_mask(meta, first, rows)).astype(bf16)
    result = resid[...].astype(f32) + summed[:, 0:MODEL_WIDTH] + mm(mid, up_out[...])
    select = pack_matrix(key_col[...], key_row[...])
    sent_out[...] = mm(select, result.astype(bf16)).astype(bf16)
    gup_out[...] = mm(mid, cotangent[...], TN)


def input_grad_kernel(key_col, key_row, resid, own, other, cotangent, gain, sent_out):
    values = resid[...].astype(f32)
    scale = lax.rsqrt(jnp.mean(values * values, axis=1, keepdims=True) + epsilon)
    weighted = (own[...].astype(f32) + other[...].astype(f32)) * gain[...]
    inner = jnp.mean(weighted * values, axis=1, keepdims=True)
    grad = scale * (weighted - values * (scale * scale * inner))
    result = cotangent[...].astype(f32) + grad
    select = pack_matrix(key_col[...], key_row[...])
    sent_out[...] = mm(select, result.astype(bf16)).astype(bf16)


def finish_kernel(
    key_col, key_row, rows, total, rows_out, gdown_in, gup, gup_rest, gdown_out, gup_out
):
    select = unpack_matrix(key_col[...], key_row[...])
    rows_out[...] = mm(select, rows[...]).astype(bf16)
    inner = gup.shape[2]
    rest_at = 2 * MODEL_WIDTH
    zx_at = rest_at + REST_LOCAL
    out_at = zx_at + 2 * inner
    for first, out in ((0, gdown_in), (out_at, gdown_out)):
        for tile in range(out.shape[0] // LANES):
            span = slice(tile * LANES, (tile + 1) * LANES)
            out[span, :] = total[:, first + tile * LANES : first + (tile + 1) * LANES].astype(f32)
    gup_out[...] = total[:, MODEL_WIDTH:rest_at].astype(f32)
    columns = gup_rest.shape[0]
    for first in range(0, columns, LANES):
        turned = total[:, rest_at + first : rest_at + first + LANES].astype(f32).T
        count = min(LANES, columns - first)
        gup_rest[first : first + count, :] = turned[0:count, :]
    gup[:, 0, :] = total[:, zx_at : zx_at + inner].astype(f32)
    gup[:, 1, :] = total[:, zx_at + inner : out_at].astype(f32)


def body(
    tokens,
    cotangent,
    lengths,
    sequence_adapter,
    perm,
    dealt_position,
    block_norm_gain,
    gate_input_weight,
    rest_weight,
    filter_taps_input,
    filter_taps_bc,
    step_bias,
    head_decay_rate,
    skip_weight,
    gated_norm_gain,
    output_weight,
    adapter_down_in,
    adapter_up_gate_input,
    adapter_up_rest,
    adapter_down_out,
    adapter_up_out,
):
    tensor_count = lax.axis_size("tensor")
    tok_dev = tokens.shape[0]
    group_rows = tok_dev * tensor_count
    heads = step_bias.shape[0]
    inner = heads * HEADDIM
    inner_all = inner * tensor_count
    dp_rank = lax.axis_index("dp")
    tensor_rank = lax.axis_index("tensor")
    dp_count = lax.axis_size("dp")
    swap = [(0, 1), (1, 0)]

    def deal(rows):
        return lax.all_to_all(rows, "dp", split_axis=0, concat_axis=0, tiled=True)

    pairwise = tensor_count == 2
    block = min(BLOCK, group_rows)
    block_count = group_rows // block
    half_count = block_count // 2 if pairwise else block_count

    def gather_rows(mine):
        if pairwise:
            return mine, lax.ppermute(mine, "tensor", swap)
        full = lax.all_gather(mine, "tensor", axis=0, tiled=True)
        return full, full

    def own_rows(full, axis=0):
        return lax.dynamic_slice_in_dim(full, tensor_rank * tok_dev, tok_dev, axis)

    def sum_tensor(values):
        if pairwise:
            return values + lax.ppermute(values, "tensor", swap)
        return lax.psum(values, "tensor")

    def scatter_rows(full):
        summed = lax.psum_scatter(full.astype(f32), "tensor", scatter_dimension=0, tiled=True)
        return summed, jnp.zeros_like(summed)

    bits = [1 << k for k in range(dp_count.bit_length() - 1)]

    def exchange(values, bit):
        pairs = [(k, k ^ bit) for k in range(dp_count)]
        return lax.ppermute(values.astype(bf16), "dp", pairs)

    def sum_dp(values, after):
        height = values.shape[0] // dp_count
        for bit, other_work in zip(bits, [None, *after] + [None] * len(bits)):
            if other_work is not None:
                values, _ = lax.optimization_barrier((values, other_work))
            pairs = values.reshape(values.shape[0] // (2 * height), 2, height, values.shape[1])
            mine = (dp_rank // bit) % 2
            pick = lambda side: lax.dynamic_index_in_dim(pairs, side, 1, keepdims=False).reshape(
                values.shape[0] // 2, values.shape[1]
            )
            values = pick(mine) + exchange(pick(1 - mine), bit).astype(f32)
        return values

    def spread_dp(share):
        return lax.all_gather(share.astype(bf16), "dp", axis=0, tiled=True)

    group_lens = lax.dynamic_slice_in_dim(lengths, dp_rank * SEQ_GROUP, SEQ_GROUP)
    starts = jnp.cumsum(group_lens) - group_lens
    group_ids = lax.dynamic_slice_in_dim(sequence_adapter, dp_rank * SEQ_GROUP, SEQ_GROUP)
    placing = jnp.stack(
        [
            jnp.int32(half_count),
            tensor_rank if pairwise else jnp.int32(0),
            tensor_rank * tok_dev,
            1 - tensor_rank if pairwise else jnp.int32(0),
        ]
    )
    meta = jnp.concatenate([starts, group_ids, placing]).astype(jnp.int32)
    slot = jnp.arange(tok_dev, dtype=jnp.int32)
    given_key = (perm // group_rows) * tok_dev + slot
    dealt_key = (dealt_position // group_rows) * tok_dev + slot

    def keys(values):
        return values[:, None], values[None, :]

    token_rows = jax.ShapeDtypeStruct((tok_dev, MODEL_WIDTH), bf16)
    move_flops = 2 * tok_dev * tok_dev * MODEL_WIDTH
    gain_row = block_norm_gain[None, :]

    dt_start = 2 * STATE + tensor_rank * heads

    def local_rest(matrix):
        steps = lax.dynamic_slice_in_dim(matrix, dt_start, heads, 1)
        return jnp.concatenate(
            [matrix[:, : 2 * STATE], jnp.pad(steps, ((0, 0), (0, LANES - heads)))], axis=1
        )

    def gather_weight(*shards):
        return lax.all_gather(jnp.concatenate(shards, axis=1), "dp", axis=0, tiled=True)

    w_in = gather_weight(
        gate_input_weight[:, 1, :], gate_input_weight[:, 0, :], local_rest(rest_weight)
    )
    w_out = gather_weight(output_weight.T)
    up_rest = local_rest(adapter_up_rest)
    up_gate = adapter_up_gate_input[:, 0, :]
    up_x = adapter_up_gate_input[:, 1, :]
    taps = jnp.pad(filter_taps_input, ((0, 3), (0, 0)))
    taps_bc = jnp.pad(filter_taps_bc, ((0, 3), (0, 0)))
    head_row = lambda values: jnp.pad(values, (0, LANES - heads))[None, :]
    bias_row, decay_row = head_row(step_bias), head_row(head_decay_rate)
    skip_row = jnp.repeat(skip_weight, HEADDIM)[None, :]
    indicator = jnp.asarray(np.arange(inner)[:, None] // HEADDIM == np.arange(LANES)[None, :], bf16)

    sent_tokens, sent_cotangent = simple_call(
        pack_kernel, (token_rows, token_rows), 2 * move_flops, *keys(dealt_position), tokens, cotangent
    )
    resid, normed_mine = simple_call(
        place_norm_kernel, (token_rows, token_rows), move_flops,
        *keys(given_key), deal(sent_tokens), gain_row,
    )
    normed = gather_rows(normed_mine)
    grad_mine = simple_call(
        unpack_kernel, token_rows, move_flops, *keys(given_key), deal(sent_cotangent)
    )
    grad_full = gather_rows(grad_mine)

    gated_gain = gated_norm_gain[None, :]
    x_act, slope, scan_out, gate_pre, gained, states, bc, dbc, dt, sig, mid_in, square = forward_scan(
        meta, normed, w_in, adapter_down_in, up_x, up_rest, up_gate, taps, taps_bc,
        bias_row, decay_row, skip_row, gated_gain, heads, group_rows, block,
    )
    weighted, gmid, stats = out_grad(
        meta, grad_full, gained, square, w_out, adapter_down_out, adapter_up_out, gated_gain, pairwise
    )
    half_rows = tok_dev if pairwise else group_rows
    gained, _ = lax.optimization_barrier((gained, stats))
    part_sent, part_own = out_project(meta, gained, w_out, adapter_down_out, half_rows)
    stats = sum_tensor(stats)
    if pairwise:
        part_sent, stats = lax.optimization_barrier((part_sent, stats))
        part_other = lax.ppermute(part_sent, "tensor", swap)
    else:
        part_own, part_other = scatter_rows(part_sent)

    gz, grest, gmid_in, gradients = backward_scan(
        meta, scan_out, gate_pre, weighted, x_act, slope, bc, dbc, dt, sig, states, stats,
        normed, mid_in, gained, gmid, taps, taps_bc, decay_row, skip_row, indicator,
        up_gate, up_x, up_rest, heads, inner_all, block,
    )
    part_other, _ = lax.optimization_barrier((part_other, gz))
    sent_output, gup_out = simple_call(
        partial(output_kernel, inner_all=inner_all),
        (token_rows, jax.ShapeDtypeStruct((LANES, MODEL_WIDTH), f32)), 2 * move_flops,
        meta, *keys(perm), resid, part_own, part_other,
        own_rows(stats, 1), grad_mine, adapter_up_out, scalars=1,
    )
    dealt_output = deal(sent_output)
    gradients = lax.dynamic_update_slice(gradients, gup_out, (0, MODEL_WIDTH))
    gz, _ = lax.optimization_barrier((gz, gradients))
    back = partial(project_back, meta, gz, grest, gmid_in, w_in, adapter_down_in, half_rows)
    if pairwise:
        sent_back = back(0)
        grad_other = lax.ppermute(sent_back, "tensor", swap)
        gz, _, dealt_output = lax.optimization_barrier((gz, sent_back, dealt_output))
        grad_own = project_back(meta, gz, grest, gmid_in, w_in, adapter_down_in, half_rows, 1)
    else:
        grad_own, grad_other = scatter_rows(back(0))
    output = simple_call(unpack_kernel, token_rows, move_flops, *keys(dealt_key), dealt_output)
    grad_other, output = lax.optimization_barrier((grad_other, output))
    sent_grad = simple_call(
        input_grad_kernel, token_rows, move_flops,
        *keys(perm), resid, grad_own, grad_other, grad_mine, gain_row,
    )

    rest_at = 2 * MODEL_WIDTH
    zx_at = rest_at + REST_LOCAL
    out_at = zx_at + 2 * inner
    total = sum_dp(gradients, (sent_back, grad_own, grad_other) if pairwise else ())
    steps = total[:, rest_at + 2 * STATE : rest_at + 2 * STATE + heads]
    wide = jnp.zeros((total.shape[0], LANES), f32)
    wide = lax.dynamic_update_slice(wide, steps, (0, tensor_rank * heads))
    shared = jnp.concatenate([total[:, : rest_at + 2 * STATE], wide], axis=1)
    share = jnp.concatenate([sum_tensor(shared), total[:, zx_at:]], axis=1)
    share, sent_grad = lax.optimization_barrier((share, sent_grad))
    total = spread_dp(share)
    dealt_grad = deal(sent_grad)
    input_grad, gdown_in, gup_zx, gup_rest, gdown_out, gup_out = simple_call(
        finish_kernel,
        (
            token_rows,
            jax.ShapeDtypeStruct((MODEL_WIDTH, LANES), f32),
            jax.ShapeDtypeStruct((LANES, 2, inner), f32),
            jax.ShapeDtypeStruct((adapter_up_rest.shape[1], LANES), f32),
            jax.ShapeDtypeStruct((inner, LANES), f32),
            jax.ShapeDtypeStruct((LANES, MODEL_WIDTH), f32),
        ),
        move_flops, *keys(dealt_key), dealt_grad, total,
    )
    return output, input_grad, gdown_in, gup_zx, gup_rest.T, gdown_out, gup_out


def solution(mesh):
    placed = (
        P(("dp", "tensor"), None),
        P(("dp", "tensor"), None),
        P(),
        P(),
        P(("dp", "tensor")),
        P(("dp", "tensor")),
        P(),
        P("dp", None, "tensor"),
        P("dp", None),
        P(None, "tensor"),
        P(),
        P("tensor"),
        P("tensor"),
        P("tensor"),
        P("tensor"),
        P("tensor", "dp"),
        P(),
        P(None, None, "tensor"),
        P(),
        P("tensor", None),
        P(),
    )
    return jax.shard_map(
        body,
        mesh=mesh,
        in_specs=placed,
        out_specs=(
            P(("dp", "tensor"), None),
            P(("dp", "tensor"), None),
            P(),
            P(None, None, "tensor"),
            P(),
            P("tensor", None),
            P(),
        ),
        check_vma=False,
    )
```

```python
from functools import partial

import jax
import jax.numpy as jnp
import numpy as np
from jax import lax
from jax.experimental import pallas as pl
from jax.experimental.pallas import tpu as pltpu
from jax.sharding import PartitionSpec as P

MODEL_WIDTH = 1536
HEADDIM = 64
STATE = 128
LANES = 128
CHUNK = 128
BLOCK = 256
ADAPTER_RANK = 16
SEQ_GROUP = 4
REST_LOCAL = 2 * STATE + LANES
META_HALF = 2 * SEQ_GROUP
META_RANK = META_HALF + 1
META_FIRST = META_HALF + 2
META_THEIRS = META_HALF + 3
COLUMNS = 512

epsilon = 1e-05
LOG2E = 1.4426950408889634
VMEM_BYTES = 56 * 1024 * 1024
f32 = jnp.float32
bf16 = jnp.bfloat16

NN = (((1,), (0,)), ((), ()))
NT = (((1,), (1,)), ((), ()))
TN = (((0,), (0,)), ((), ()))


def mm(left, right, dims=NN):
    return lax.dot_general(left, right, dims, preferred_element_type=f32)


def params(count=1):
    return pltpu.CompilerParams(
        dimension_semantics=("arbitrary",) * count, vmem_limit_bytes=VMEM_BYTES
    )


def whole(shape):
    return pl.BlockSpec(shape, lambda *_: (0,) * len(shape))


def iota(shape, axis):
    return lax.broadcasted_iota(jnp.int32, shape, axis)


def pack_matrix(key_col, key_row):
    count = key_row.shape[1]
    rank = jnp.sum((key_col < key_row).astype(f32), axis=0, keepdims=True).astype(jnp.int32)
    return (iota((count, count), 0) == rank).astype(f32).astype(bf16)


def unpack_matrix(key_col, key_row):
    count = key_row.shape[1]
    rank = jnp.sum((key_row < key_col).astype(f32), axis=1, keepdims=True).astype(jnp.int32)
    return (iota((count, count), 1) == rank).astype(f32).astype(bf16)


def pack_kernel(key_col, key_row, first, second, first_out, second_out):
    select = pack_matrix(key_col[...], key_row[...])
    first_out[...] = mm(select, first[...]).astype(bf16)
    second_out[...] = mm(select, second[...]).astype(bf16)


def unpack_kernel(key_col, key_row, rows, rows_out):
    select = unpack_matrix(key_col[...], key_row[...])
    rows_out[...] = mm(select, rows[...]).astype(bf16)


def place_norm_kernel(key_col, key_row, rows, gain, rows_out, normed_out):
    select = unpack_matrix(key_col[...], key_row[...])
    resid = mm(select, rows[...])
    rows_out[...] = resid.astype(bf16)
    scale = lax.rsqrt(jnp.mean(resid * resid, axis=1, keepdims=True) + epsilon)
    normed_out[...] = (resid * scale * gain[...]).astype(bf16)


def simple_call(kernel, outs, flops, *args, scalars=0):
    vector = pl.BlockSpec(memory_space=pltpu.VMEM)
    scalar = pl.BlockSpec(memory_space=pltpu.SMEM)
    return pl.pallas_call(
        kernel,
        out_shape=outs,
        in_specs=[scalar] * scalars + [vector] * (len(args) - scalars),
        out_specs=jax.tree.map(lambda _: vector, outs),
        compiler_params=pltpu.CompilerParams(vmem_limit_bytes=VMEM_BYTES),
        cost_estimate=pl.CostEstimate(flops=flops, bytes_accessed=1_000_000, transcendentals=0),
    )(*args)


def segment_start(meta, position):
    begin = jnp.zeros_like(position)
    for k in range(1, SEQ_GROUP):
        begin = jnp.where(position >= meta[k], meta[k], begin)
    return begin


def row_specs(block, width, place, scale=1):
    def spec(side):
        def index(i, meta):
            half = meta[META_HALF] * scale
            return (jnp.clip(place(i, meta) - meta[side] * half, 0, half - 1), 0)

        return pl.BlockSpec((block, width), index)

    return [spec(META_RANK), spec(META_THEIRS)]


def pick_rows(meta, place, mine, other, scale=1):
    own = place // (meta[META_HALF] * scale) == meta[META_RANK]
    return jnp.where(own, mine[...], other[...])


def adapter_mask(meta, first, rows):
    position = first + iota((rows, LANES), 0)
    owner = jnp.full((rows, LANES), meta[SEQ_GROUP], jnp.int32)
    for k in range(1, SEQ_GROUP):
        owner = jnp.where(position >= meta[k], meta[SEQ_GROUP + k], owner)
    return (iota((rows, LANES), 1) // ADAPTER_RANK == owner).astype(f32)


def cumulate(values):
    total = values
    step = 1
    while step < values.shape[0]:
        pad = jnp.zeros((step, values.shape[1]), f32)
        total = total + jnp.concatenate([pad, total[:-step]], axis=0)
        step *= 2
    return total


def cumulate_back(values):
    total = values
    step = 1
    while step < values.shape[0]:
        pad = jnp.zeros((step, values.shape[1]), f32)
        total = total + jnp.concatenate([total[step:], pad], axis=0)
        step *= 2
    return total


def sigmoid(values):
    return 0.5 * jnp.tanh(0.5 * values) + 0.5


def column(values, h):
    return jnp.broadcast_to(values[:, h : h + 1], (values.shape[0], LANES))


def decay_tables(dt, decay_rate):
    cumul = cumulate(dt * (-LOG2E * decay_rate))
    source = cumul - jnp.log(jnp.maximum(dt, 1e-37)) * LOG2E
    return cumul, source


def forward_kernel(
    meta,
    mine, other, w_in, down_in, up_x, up_rest, up_gate, taps, taps_bc, step_bias, decay_rate, skip, gain,
    x_out, dx_out, y_out, gate_out, gained_out, state_out, bc_out, dbc_out, dt_out, sig_out, mid_out,
    square_out,
    conv_in, rest, gate_pre, state, from_state, scaled,
    *, heads, block,
):
    i = pl.program_id(0)
    inner = heads * HEADDIM
    per_block = block // CHUNK
    first = i * CHUNK

    @pl.when(i == 0)
    def _():
        conv_in[block : block + 8, :] = jnp.zeros((8, inner), f32)
        rest[block : block + 8, :] = jnp.zeros((8, REST_LOCAL), f32)
        state[...] = jnp.zeros_like(state)

    @pl.when(i % per_block == 0)
    def _():
        conv_in[0:8, :] = conv_in[block : block + 8, :]
        rest[0:8, :] = rest[block : block + 8, :]
        rows = pick_rows(meta, i // per_block, mine, other)
        mid = (mm(rows, down_in[...]) * adapter_mask(meta, first, block)).astype(bf16)
        mid_out[...] = mid
        conv_in[8 : block + 8, :] = mm(rows, w_in[:, 0:inner]) + mm(mid, up_x[...])
        gate_pre[...] = mm(rows, w_in[:, inner : 2 * inner]) + mm(mid, up_gate[...])
        rest[8 : block + 8, :] = mm(rows, w_in[:, 2 * inner :]) + mm(mid, up_rest[...])

    offset = pl.multiple_of((i % per_block) * CHUNK, CHUNK)
    window = pl.ds(offset, CHUNK + 8)
    position = first + iota((CHUNK, LANES), 0)
    begin = segment_start(meta, position)
    depth = position - begin
    same = [(depth >= k).astype(f32) for k in (1, 2, 3)]

    def conv(ext, tap):
        summed = tap[3:4] * ext[8:] + tap[4:5]
        for k in (1, 2, 3):
            summed = summed + tap[3 - k : 4 - k] * (ext[8 - k : 8 - k + CHUNK] * same[k - 1])
        sig = sigmoid(summed)
        act = summed * sig
        return act, sig + act * (1.0 - sig)

    b_act, b_slope = conv(rest[window, 0:STATE], taps_bc[:, 0:STATE])
    c_act, c_slope = conv(rest[window, STATE : 2 * STATE], taps_bc[:, STATE : 2 * STATE])
    b_mat = b_act.astype(bf16)
    c_mat = c_act.astype(bf16)
    bc_out[:, 0:STATE] = b_mat
    bc_out[:, STATE : 2 * STATE] = c_mat
    dbc_out[:, 0:STATE] = b_slope
    dbc_out[:, STATE : 2 * STATE] = c_slope
    step_pre = rest[window, 2 * STATE : REST_LOCAL][8:] + step_bias[...]
    dt = jnp.maximum(step_pre, 0.0) + jnp.log(1.0 + jnp.exp(-jnp.abs(step_pre)))
    small = jnp.exp(step_pre)
    dt = jnp.where(step_pre < -8.0, small * (1.0 - 0.5 * small), dt)
    dt_out[...] = dt
    sig_out[...] = sigmoid(step_pre)
    cumul, source = decay_tables(dt, decay_rate[...])
    source_rows = source.T
    total = cumul[CHUNK - 1 : CHUNK, :]
    s_pos = first + iota((CHUNK, CHUNK), 1)
    allowed = jnp.where((s_pos <= position) & (s_pos >= begin), 0.0, -1e30)
    scores = mm(c_mat, b_mat, NT)
    begin_last = segment_start(meta, first + CHUNK - 1)
    kept = jnp.where(begin_last < first, 1.0, 0.0)
    in_last = (position >= begin_last).astype(f32)
    carried = (begin < first).astype(f32)
    state_low = state[...].astype(bf16)
    state_out[...] = state_low
    from_state[...] = mm(c_mat, state_low)
    left = iota((CHUNK, LANES), 1) < HEADDIM
    left_row = left[0:1]
    square = jnp.zeros((CHUNK, LANES), f32)
    for pair in range(heads // 2):
        h0, h1 = 2 * pair, 2 * pair + 1
        cols = slice(pair * LANES, (pair + 1) * LANES)
        act, slope = conv(conv_in[window, cols], taps[:, cols])
        x_low = act.astype(bf16)
        x_out[:, cols] = x_low
        dx_out[:, cols] = slope.astype(bf16)
        x = x_low.astype(f32)
        cum0, cum1 = column(cumul, h0), column(cumul, h1)
        m0 = jnp.exp2(cum0 - source_rows[h0 : h0 + 1] + allowed) * scores
        m1 = jnp.exp2(cum1 - source_rows[h1 : h1 + 1] + allowed) * scores
        weights = jnp.concatenate([m0.astype(bf16), m1.astype(bf16)], axis=1)
        x_split = jnp.concatenate(
            [jnp.where(left, x, 0.0).astype(bf16), jnp.where(left, 0.0, x).astype(bf16)], axis=0
        )
        inside = mm(weights, x_split)
        reach = jnp.exp2(jnp.where(left, cum0, cum1)) * carried
        y = inside + reach * from_state[:, cols] + skip[:, cols] * x
        y_out[:, cols] = y
        gate = gate_pre[pl.ds(offset, CHUNK), cols]
        gate_out[:, cols] = gate
        gated = y * (gate * sigmoid(gate))
        square = square + gated * gated
        gained_out[:, cols] = (gated * gain[:, cols]).astype(bf16)
        total_pair = jnp.where(left_row, column(total, h0), column(total, h1))
        source_pair = jnp.where(left, column(source, h0), column(source, h1))
        coefficient = jnp.exp2(total_pair - source_pair) * in_last
        scaled[:, cols] = (x * coefficient).astype(bf16)
        state[:, cols] = state[:, cols] * (jnp.exp2(total_pair) * kept)
    state[...] += mm(b_mat, scaled[...], TN)
    square_out[...] = jnp.sum(square.T, axis=0, keepdims=True)


def forward_scan(meta, normed, w_in, down_in, up_x, up_rest, up_gate, taps, taps_bc, bias, decay, skip, gain, heads, rows, block):
    inner = heads * HEADDIM
    per_block = block // CHUNK
    chunk_rows = lambda width: pl.BlockSpec((CHUNK, width), lambda i, *_: (i, 0))
    block_rows = lambda width: pl.BlockSpec((block, width), lambda i, *_: (i // per_block, 0))
    outs = (
        jax.ShapeDtypeStruct((rows, inner), bf16),
        jax.ShapeDtypeStruct((rows, inner), bf16),
        jax.ShapeDtypeStruct((rows, inner), f32),
        jax.ShapeDtypeStruct((rows, inner), f32),
        jax.ShapeDtypeStruct((rows, inner), bf16),
        jax.ShapeDtypeStruct((rows // CHUNK * STATE, inner), bf16),
        jax.ShapeDtypeStruct((rows, 2 * STATE), bf16),
        jax.ShapeDtypeStruct((rows, 2 * STATE), f32),
        jax.ShapeDtypeStruct((rows, LANES), f32),
        jax.ShapeDtypeStruct((rows, LANES), f32),
        jax.ShapeDtypeStruct((rows, LANES), bf16),
        jax.ShapeDtypeStruct((1, rows), f32),
    )
    operands = (w_in, down_in, up_x, up_rest, up_gate, taps, taps_bc, bias, decay, skip, gain)
    grid = pltpu.PrefetchScalarGridSpec(
        num_scalar_prefetch=1,
        grid=(rows // CHUNK,),
        in_specs=row_specs(block, MODEL_WIDTH, lambda i, meta: i // per_block)
        + [whole(a.shape) for a in operands],
        out_specs=[
            chunk_rows(inner), chunk_rows(inner), chunk_rows(inner), chunk_rows(inner),
            chunk_rows(inner), chunk_rows(inner),
            chunk_rows(2 * STATE), chunk_rows(2 * STATE), chunk_rows(LANES), chunk_rows(LANES),
            block_rows(LANES), pl.BlockSpec((1, CHUNK), lambda i, *_: (0, i)),
        ],
        scratch_shapes=[
            pltpu.VMEM((block + 8, inner), f32),
            pltpu.VMEM((block + 8, REST_LOCAL), f32),
            pltpu.VMEM((block, inner), f32),
            pltpu.VMEM((STATE, inner), f32),
            pltpu.VMEM((CHUNK, inner), f32),
            pltpu.VMEM((CHUNK, inner), bf16),
        ],
    )
    return pl.pallas_call(
        partial(forward_kernel, heads=heads, block=block),
        out_shape=outs,
        grid_spec=grid,
        compiler_params=params(),
        cost_estimate=pl.CostEstimate(
            flops=5 * rows * MODEL_WIDTH * inner, bytes_accessed=50_000_000, transcendentals=0
        ),
    )(meta, *normed, *operands)


def out_grad_kernel(
    meta,
    gd_mine, gd_other, gained, square, w_out, down_out, up_out, gain,
    weighted_out, gmid_out, stats_out,
    gd, cross,
    *, pairwise,
):
    step = pl.program_id(0)
    rows = gd.shape[0]

    @pl.when(step == 0)
    def _():
        if pairwise:
            tokens = gd_mine.shape[0]
            gd[pl.ds(pl.multiple_of(meta[META_FIRST], LANES), tokens), :] = gd_mine[...]
            gd[pl.ds(pl.multiple_of(rows - tokens - meta[META_FIRST], LANES), tokens), :] = gd_other[...]
        else:
            gd[...] = gd_mine[...]
        gmid = mm(gd[...], up_out[...], NT) * adapter_mask(meta, 0, rows)
        gmid_out[...] = gmid.astype(bf16)
        cross[...] = jnp.zeros_like(cross)

    grad = mm(gd[...], w_out[...]) + mm(gmid_out[...], down_out[...], NT)
    weighted_out[...] = grad * gain[...]
    product = grad * gained[...].astype(f32)
    total = cross[...]
    for tile in range(product.shape[1] // LANES):
        total = total + product[:, tile * LANES : (tile + 1) * LANES]
    cross[...] = total

    @pl.when(step == pl.num_programs(0) - 1)
    def _():
        row = jnp.sum(cross[...].T, axis=0, keepdims=True)
        stats_out[...] = jnp.where(iota((8, rows), 0) == 0, square[...], row)


def out_grad(meta, cotangent, gained, square, w_out, down_out, up_out, gain, pairwise):
    rows, inner = gained.shape
    width = 4 * LANES if inner % (4 * LANES) == 0 else LANES
    columns = lambda height: pl.BlockSpec((height, width), lambda i, *_: (0, i))
    outs = (
        jax.ShapeDtypeStruct((rows, inner), f32),
        jax.ShapeDtypeStruct((rows, LANES), bf16),
        jax.ShapeDtypeStruct((8, rows), f32),
    )
    grid = pltpu.PrefetchScalarGridSpec(
        num_scalar_prefetch=1,
        grid=(inner // width,),
        in_specs=[
            whole(cotangent[0].shape), whole(cotangent[1].shape), columns(rows), whole(square.shape),
            columns(MODEL_WIDTH), pl.BlockSpec((width, LANES), lambda i, *_: (i, 0)),
            whole(up_out.shape), columns(1),
        ],
        out_specs=[columns(rows), whole(outs[1].shape), whole(outs[2].shape)],
        scratch_shapes=[pltpu.VMEM((rows, MODEL_WIDTH), bf16), pltpu.VMEM((rows, LANES), f32)],
    )
    return pl.pallas_call(
        partial(out_grad_kernel, pairwise=pairwise),
        out_shape=outs,
        grid_spec=grid,
        compiler_params=params(),
        cost_estimate=pl.CostEstimate(
            flops=2 * rows * MODEL_WIDTH * inner, bytes_accessed=20_000_000, transcendentals=0
        ),
    )(meta, *cotangent, gained, square, w_out, down_out, up_out, gain)


def halves(meta_rows, width):
    theirs = pl.BlockSpec((meta_rows, width), lambda i, meta: (meta[META_THEIRS], 0))
    own = pl.BlockSpec((meta_rows, width), lambda i, meta: (meta[META_RANK], 0))
    return theirs, own


def out_project_kernel(meta, theirs, own, w_out, down_out, sent_out, kept_out):
    step = pl.program_id(0)
    width = w_out.shape[0]
    columns = pl.ds(pl.multiple_of(step * width, LANES), width)
    sent_out[:, columns] = mm(theirs[...], w_out[...], NT).astype(bf16)
    kept_out[:, columns] = mm(own[...], w_out[...], NT).astype(bf16)

    @pl.when(step == 0)
    def _():
        sent_out[:, MODEL_WIDTH:] = mm(theirs[...], down_out[...]).astype(bf16)
        kept_out[:, MODEL_WIDTH:] = mm(own[...], down_out[...]).astype(bf16)


def out_project(meta, gained, w_out, down_out, half_rows):
    inner = gained.shape[1]
    out = jax.ShapeDtypeStruct((half_rows, MODEL_WIDTH + LANES), bf16)
    grid = pltpu.PrefetchScalarGridSpec(
        num_scalar_prefetch=1,
        grid=(MODEL_WIDTH // COLUMNS,),
        in_specs=[
            *halves(half_rows, inner),
            pl.BlockSpec((COLUMNS, inner), lambda i, *_: (i, 0)),
            whole(down_out.shape),
        ],
        out_specs=[whole(out.shape)] * 2,
    )
    return pl.pallas_call(
        out_project_kernel,
        out_shape=(out, out),
        grid_spec=grid,
        compiler_params=params(),
        cost_estimate=pl.CostEstimate(
            flops=4 * half_rows * MODEL_WIDTH * inner, bytes_accessed=15_000_000, transcendentals=0
        ),
    )(meta, gained, gained, w_out, down_out)


def split_sum(values, indicator):
    high = values.astype(bf16)
    low = (values - high.astype(f32)).astype(bf16)
    return mm(high, indicator) + mm(low, indicator)


def turn_tiles(out, first, values):
    for tile in range(values.shape[1] // LANES):
        out[:, first + tile * LANES : first + (tile + 1) * LANES] = values[
            :, tile * LANES : (tile + 1) * LANES
        ].T


def backward_kernel(
    meta,
    scan_out, gate_pre, weighted, x_in, slope_in, bc_in, dbc_in, dt_in, sig_in, state_in, stats,
    normed_mine, normed_other, mid_rows, gained, gmid_rows,
    taps, taps_bc, decay_rate, skip, indicator, up_gate, up_x, up_rest,
    gz_out, grest_out, gmid_out, grads,
    down_in, down_out, dstate, g_next, gbc_next, from_dstate, scaled, reached, product, source_product,
    *, heads, inner_all, scale,
):
    i = pl.program_id(0)
    inner = heads * HEADDIM
    place = pl.num_programs(0) - 1 - i
    first = place * CHUNK
    rest_at = 2 * MODEL_WIDTH
    zx_at = rest_at + REST_LOCAL
    out_at = zx_at + 2 * inner

    @pl.when(i == 0)
    def _():
        dstate[...] = jnp.zeros_like(dstate)
        g_next[...] = jnp.zeros_like(g_next)
        gbc_next[...] = jnp.zeros_like(gbc_next)
        product[CHUNK:, :] = jnp.zeros((8, inner), f32)
        grads[...] = jnp.zeros_like(grads)
        down_in[...] = jnp.zeros_like(down_in)
        down_out[...] = jnp.zeros_like(down_out)

    s_pos = first + iota((CHUNK, LANES), 0)
    begin = segment_start(meta, s_pos)
    long_pos = first + iota((CHUNK + 8, LANES), 0)
    long_depth = long_pos - segment_start(meta, long_pos)
    same = [(long_depth >= k).astype(f32) for k in (1, 2, 3)]
    t_pos = first + iota((CHUNK, CHUNK), 1)
    t_begin = segment_start(meta, t_pos)
    allowed = jnp.where((s_pos <= t_pos) & (s_pos >= t_begin), 0.0, -1e30)
    begin_last = segment_start(meta, first + CHUNK - 1)
    kept = jnp.where(begin_last < first, 1.0, 0.0)
    in_last = (s_pos >= begin_last).astype(f32)
    carried = (begin < first).astype(f32)

    factor = lax.rsqrt(stats[0:1, :] * (1.0 / inner_all) + epsilon)
    pull = factor * factor * factor * stats[1:2, :] * (1.0 / inner_all)
    row_id = iota((LANES, CHUNK), 0)
    both = jnp.where(row_id == 0, factor, jnp.where(row_id == 1, pull, 0.0)).T
    factor_col, pull_col = column(both, 0), column(both, 1)
    gmid_scaled = (gmid_rows[...].astype(f32) * factor_col).astype(bf16)
    down_out[...] += mm(gmid_scaled, gained[...], TN)
    mid_turned = mid_rows[...].astype(f32).T.astype(bf16)

    dt = dt_in[...]
    sig = sig_in[...]
    cumul, source = decay_tables(dt, decay_rate[...])
    cumul_rows = cumul.T
    total = cumul[CHUNK - 1 : CHUNK, :]
    b_mat = bc_in[:, 0:STATE]
    c_mat = bc_in[:, STATE : 2 * STATE]
    scores = mm(b_mat, c_mat, NT)
    dstate_low = dstate[...].astype(bf16)
    from_dstate[...] = mm(b_mat, dstate_low)
    left = iota((CHUNK, LANES), 1) < HEADDIM
    left_row = left[0:1]
    gscores = jnp.zeros((CHUNK, CHUNK), f32)

    def conv_back(grad, later, tap):
        ext = jnp.concatenate([grad, later], axis=0)
        out = tap[3:4] * grad
        for k in (1, 2, 3):
            out = out + tap[3 - k : 4 - k] * (ext * same[k - 1])[k : k + CHUNK]
        return out

    for pair in range(heads // 2):
        h0, h1 = 2 * pair, 2 * pair + 1
        cols = slice(pair * LANES, (pair + 1) * LANES)
        gate = gate_pre[:, cols]
        y = scan_out[:, cols]
        gate_sig = sigmoid(gate)
        silu = gate * gate_sig
        ggated = weighted[:, cols] * factor_col - y * silu * pull_col
        gy_low = (ggated * silu).astype(bf16)
        ggate = (ggated * y * (gate_sig + silu * (1.0 - gate_sig))).astype(bf16)
        gz_out[:, cols] = ggate
        gy = gy_low.astype(f32)
        gy_split = jnp.concatenate(
            [jnp.where(left, gy, 0.0).astype(bf16), jnp.where(left, 0.0, gy).astype(bf16)], axis=0
        )
        x_low = x_in[:, cols]
        x = x_low.astype(f32)
        dots = mm(x_low, gy_split, NT)
        src0, src1 = column(source, h0), column(source, h1)
        e0 = jnp.exp2(cumul_rows[h0 : h0 + 1] - src0 + allowed)
        e1 = jnp.exp2(cumul_rows[h1 : h1 + 1] - src1 + allowed)
        gscores = gscores + dots[:, 0:CHUNK] * e0 + dots[:, CHUNK:] * e1
        weights = jnp.concatenate([(e0 * scores).astype(bf16), (e1 * scores).astype(bf16)], axis=1)
        inside = mm(weights, gy_split)
        total_pair = jnp.where(left_row, column(total, h0), column(total, h1))
        coefficient = jnp.exp2(total_pair - jnp.where(left, src0, src1)) * in_last
        reach = jnp.exp2(jnp.where(left, column(cumul, h0), column(cumul, h1))) * carried
        outside = coefficient * from_dstate[:, cols]
        gx_scan = inside + outside
        skip_row = skip[:, cols]
        gx = gx_scan + skip_row * gy
        x_side = x * gx_scan
        source_product[:, cols] = x_side.astype(bf16)
        product[0:CHUNK, cols] = gy * (y - skip_row * x) - x_side
        scaled[:, cols] = (x * coefficient).astype(bf16)
        reached[:, cols] = (gy * reach).astype(bf16)
        keep_row = jnp.exp2(total_pair) * kept
        dstate_cols = dstate[:, cols]
        product[CHUNK : CHUNK + 1, cols] = jnp.sum(x * outside, axis=0, keepdims=True) + keep_row * jnp.sum(
            dstate_cols * state_in[:, cols].astype(f32), axis=0, keepdims=True
        )
        dstate[:, cols] = dstate_cols * keep_row
        gconv = gx * slope_in[:, cols].astype(f32)
        later = slice(inner + pair * LANES, inner + (pair + 1) * LANES)
        gconv_in = conv_back(gconv, g_next[:, cols], taps[:, cols]).astype(bf16)
        gz_out[:, later] = gconv_in
        g_next[:, cols] = gconv[0:8]

    gscores_low = gscores.astype(bf16)
    grad_b = mm(gscores_low, c_mat) + mm(scaled[...], dstate_low, NT)
    grad_c = mm(gscores_low, b_mat, TN) + mm(reached[...], state_in[...], NT)
    for part, grad in ((0, grad_b), (1, grad_c)):
        cols = slice(part * STATE, (part + 1) * STATE)
        gconv = grad * dbc_in[:, cols]
        grest_out[:, cols] = conv_back(gconv, gbc_next[:, cols], taps_bc[:, cols]).astype(bf16)
        gbc_next[:, cols] = gconv[0:8]
    dstate[...] += mm(c_mat, reached[...], TN)

    sums = split_sum(product[...], indicator[...])
    direct = mm(source_product[...], indicator[...])
    grad_log = cumulate_back(sums[0:CHUNK]) + sums[CHUNK : CHUNK + 1]
    ratio = jnp.where(dt > 1e-30, sig / jnp.maximum(dt, 1e-30), 1.0)
    grad_pre = direct * ratio - decay_rate[...] * grad_log * sig
    used = iota((CHUNK, LANES), 1) < heads
    grest_out[:, 2 * STATE : REST_LOCAL] = jnp.where(used, grad_pre, 0.0).astype(bf16)

    grest = grest_out[...]
    gmid = mm(gz_out[:, 0:inner], up_gate[...], NT) + mm(gz_out[:, inner:], up_x[...], NT)
    gmid = gmid + mm(grest, up_rest[...], NT)
    grads[:, zx_at:out_at] += mm(mid_turned, gz_out[...])
    gmid = (gmid * adapter_mask(meta, first, CHUNK)).astype(bf16)
    gmid_out[...] = gmid
    grads[:, rest_at:zx_at] += mm(mid_turned, grest)
    down_in[...] += mm(gmid, pick_rows(meta, place, normed_mine, normed_other, scale), TN)

    @pl.when(place == 0)
    def _():
        turn_tiles(grads, 0, down_in[...])
        turn_tiles(grads, out_at, down_out[...])


def backward_scan(meta, scan_out, gate_pre, weighted, x_act, slope, bc, dbc, dt, sig, states, stats, normed, mid, gained, gmid, taps, taps_bc, decay, skip, indicator, up_gate, up_x, up_rest, heads, inner_all, block):
    rows, inner = scan_out.shape
    count = rows // CHUNK
    chunk_rows = lambda width: pl.BlockSpec((CHUNK, width), lambda i, *_: (count - 1 - i, 0))
    scale = block // CHUNK
    columns = 2 * MODEL_WIDTH + REST_LOCAL + 3 * inner
    operands = (taps, taps_bc, decay, skip, indicator, up_gate, up_x, up_rest)
    streams = (scan_out, gate_pre, weighted, x_act, slope, bc, dbc, dt, sig, states)
    outs = (
        jax.ShapeDtypeStruct((rows, 2 * inner), bf16),
        jax.ShapeDtypeStruct((rows, REST_LOCAL), bf16),
        jax.ShapeDtypeStruct((rows, LANES), bf16),
        jax.ShapeDtypeStruct((LANES, columns), f32),
    )
    grid = pltpu.PrefetchScalarGridSpec(
        num_scalar_prefetch=1,
        grid=(count,),
        in_specs=[chunk_rows(a.shape[1]) for a in streams]
        + [pl.BlockSpec((8, CHUNK), lambda i, *_: (0, count - 1 - i))]
        + row_specs(CHUNK, MODEL_WIDTH, lambda i, meta: count - 1 - i, scale)
        + [chunk_rows(LANES), chunk_rows(inner), chunk_rows(LANES)]
        + [whole(a.shape) for a in operands],
        out_specs=[
            chunk_rows(2 * inner), chunk_rows(REST_LOCAL), chunk_rows(LANES), whole((LANES, columns))
        ],
        scratch_shapes=[
            pltpu.VMEM((LANES, MODEL_WIDTH), f32),
            pltpu.VMEM((LANES, inner), f32),
            pltpu.VMEM((STATE, inner), f32),
            pltpu.VMEM((8, inner), f32),
            pltpu.VMEM((8, 2 * STATE), f32),
            pltpu.VMEM((CHUNK, inner), f32),
            pltpu.VMEM((CHUNK, inner), bf16),
            pltpu.VMEM((CHUNK, inner), bf16),
            pltpu.VMEM((CHUNK + 8, inner), f32),
            pltpu.VMEM((CHUNK, inner), bf16),
        ],
    )
    return pl.pallas_call(
        partial(backward_kernel, heads=heads, inner_all=inner_all, scale=scale),
        out_shape=outs,
        grid_spec=grid,
        compiler_params=params(),
        cost_estimate=pl.CostEstimate(
            flops=6 * rows * MODEL_WIDTH * inner, bytes_accessed=50_000_000, transcendentals=0
        ),
    )(meta, *streams, stats, *normed, mid, gained, gmid, *operands)


def project_back_kernel(meta, gz, grest, gmid, w_in, down_in, grad_out, *, inner):
    grad = mm(gz[:, 0:inner], w_in[:, inner : 2 * inner], NT)
    grad = grad + mm(gz[:, inner : 2 * inner], w_in[:, 0:inner], NT)
    grad = grad + mm(grest[...], w_in[:, 2 * inner :], NT) + mm(gmid[...], down_in[...], NT)
    grad_out[...] = grad.astype(bf16)


def project_back(meta, gz, grest, gmid, w_in, down_in, half_rows, side):
    inner = gz.shape[1] // 2
    rows_of = lambda width: halves(half_rows, width)[side]
    grid = pltpu.PrefetchScalarGridSpec(
        num_scalar_prefetch=1,
        grid=(MODEL_WIDTH // COLUMNS,),
        in_specs=[
            rows_of(2 * inner), rows_of(REST_LOCAL), rows_of(LANES),
            pl.BlockSpec((COLUMNS, w_in.shape[1]), lambda i, *_: (i, 0)),
            pl.BlockSpec((COLUMNS, LANES), lambda i, *_: (i, 0)),
        ],
        out_specs=pl.BlockSpec((half_rows, COLUMNS), lambda i, *_: (0, i)),
    )
    return pl.pallas_call(
        partial(project_back_kernel, inner=inner),
        out_shape=jax.ShapeDtypeStruct((half_rows, MODEL_WIDTH), bf16),
        grid_spec=grid,
        compiler_params=params(),
        cost_estimate=pl.CostEstimate(
            flops=4 * half_rows * MODEL_WIDTH * inner, bytes_accessed=15_000_000, transcendentals=0
        ),
    )(meta, gz, grest, gmid, w_in, down_in)


def output_kernel(
    meta, key_col, key_row, resid, own, other, stats, cotangent, up_out,
    sent_out, gup_out, *, inner_all,
):
    rows = resid.shape[0]
    row_id = iota((LANES, rows), 0)
    factor = lax.rsqrt(stats[0:1, :] * (1.0 / inner_all) + epsilon)
    factor_col = jnp.where(row_id == 0, factor, 0.0).T[:, 0:1]
    first = meta[META_FIRST]
    summed = (own[...].astype(f32) + other[...].astype(f32)) * factor_col
    mid = (summed[:, MODEL_WIDTH:] * adapter_mask(meta, first, rows)).astype(bf16)
    result = resid[...].astype(f32) + summed[:, 0:MODEL_WIDTH] + mm(mid, up_out[...])
    select = pack_matrix(key_col[...], key_row[...])
    sent_out[...] = mm(select, result.astype(bf16)).astype(bf16)
    gup_out[...] = mm(mid, cotangent[...], TN)


def input_grad_kernel(key_col, key_row, resid, own, other, cotangent, gain, sent_out):
    values = resid[...].astype(f32)
    scale = lax.rsqrt(jnp.mean(values * values, axis=1, keepdims=True) + epsilon)
    weighted = (own[...].astype(f32) + other[...].astype(f32)) * gain[...]
    inner = jnp.mean(weighted * values, axis=1, keepdims=True)
    grad = scale * (weighted - values * (scale * scale * inner))
    result = cotangent[...].astype(f32) + grad
    select = pack_matrix(key_col[...], key_row[...])
    sent_out[...] = mm(select, result.astype(bf16)).astype(bf16)


def finish_kernel(
    key_col, key_row, rows, total, rows_out, gdown_in, gup, gup_rest, gdown_out, gup_out
):
    select = unpack_matrix(key_col[...], key_row[...])
    rows_out[...] = mm(select, rows[...]).astype(bf16)
    inner = gup.shape[2]
    rest_at = 2 * MODEL_WIDTH
    zx_at = rest_at + REST_LOCAL
    out_at = zx_at + 2 * inner
    for first, out in ((0, gdown_in), (out_at, gdown_out)):
        for tile in range(out.shape[0] // LANES):
            span = slice(tile * LANES, (tile + 1) * LANES)
            out[span, :] = total[:, first + tile * LANES : first + (tile + 1) * LANES].astype(f32)
    gup_out[...] = total[:, MODEL_WIDTH:rest_at].astype(f32)
    columns = gup_rest.shape[0]
    for first in range(0, columns, LANES):
        turned = total[:, rest_at + first : rest_at + first + LANES].astype(f32).T
        count = min(LANES, columns - first)
        gup_rest[first : first + count, :] = turned[0:count, :]
    gup[:, 0, :] = total[:, zx_at : zx_at + inner].astype(f32)
    gup[:, 1, :] = total[:, zx_at + inner : out_at].astype(f32)


def body(
    tokens,
    cotangent,
    lengths,
    sequence_adapter,
    perm,
    dealt_position,
    block_norm_gain,
    gate_input_weight,
    rest_weight,
    filter_taps_input,
    filter_taps_bc,
    step_bias,
    head_decay_rate,
    skip_weight,
    gated_norm_gain,
    output_weight,
    adapter_down_in,
    adapter_up_gate_input,
    adapter_up_rest,
    adapter_down_out,
    adapter_up_out,
):
    tensor_count = lax.axis_size("tensor")
    tok_dev = tokens.shape[0]
    group_rows = tok_dev * tensor_count
    heads = step_bias.shape[0]
    inner = heads * HEADDIM
    inner_all = inner * tensor_count
    dp_rank = lax.axis_index("dp")
    tensor_rank = lax.axis_index("tensor")
    dp_count = lax.axis_size("dp")
    swap = [(0, 1), (1, 0)]

    def deal(rows):
        return lax.all_to_all(rows, "dp", split_axis=0, concat_axis=0, tiled=True)

    pairwise = tensor_count == 2
    block = min(BLOCK, group_rows)
    block_count = group_rows // block
    half_count = block_count // 2 if pairwise else block_count

    def gather_rows(mine):
        if pairwise:
            return mine, lax.ppermute(mine, "tensor", swap)
        full = lax.all_gather(mine, "tensor", axis=0, tiled=True)
        return full, full

    def own_rows(full, axis=0):
        return lax.dynamic_slice_in_dim(full, tensor_rank * tok_dev, tok_dev, axis)

    def sum_tensor(values):
        if pairwise:
            return values + lax.ppermute(values, "tensor", swap)
        return lax.psum(values, "tensor")

    def scatter_rows(full):
        summed = lax.psum_scatter(full.astype(f32), "tensor", scatter_dimension=0, tiled=True)
        return summed, jnp.zeros_like(summed)

    bits = [1 << k for k in range(dp_count.bit_length() - 1)]

    def exchange(values, bit):
        pairs = [(k, k ^ bit) for k in range(dp_count)]
        return lax.ppermute(values.astype(bf16), "dp", pairs)

    def sum_dp(values, after):
        height = values.shape[0] // dp_count
        for bit, other_work in zip(bits, [None, *after] + [None] * len(bits)):
            if other_work is not None:
                values, _ = lax.optimization_barrier((values, other_work))
            pairs = values.reshape(values.shape[0] // (2 * height), 2, height, values.shape[1])
            mine = (dp_rank // bit) % 2
            pick = lambda side: lax.dynamic_index_in_dim(pairs, side, 1, keepdims=False).reshape(
                values.shape[0] // 2, values.shape[1]
            )
            values = pick(mine) + exchange(pick(1 - mine), bit).astype(f32)
        return values

    def spread_dp(share):
        return lax.all_gather(share.astype(bf16), "dp", axis=0, tiled=True)

    group_lens = lax.dynamic_slice_in_dim(lengths, dp_rank * SEQ_GROUP, SEQ_GROUP)
    starts = jnp.cumsum(group_lens) - group_lens
    group_ids = lax.dynamic_slice_in_dim(sequence_adapter, dp_rank * SEQ_GROUP, SEQ_GROUP)
    placing = jnp.stack(
        [
            jnp.int32(half_count),
            tensor_rank if pairwise else jnp.int32(0),
            tensor_rank * tok_dev,
            1 - tensor_rank if pairwise else jnp.int32(0),
        ]
    )
    meta = jnp.concatenate([starts, group_ids, placing]).astype(jnp.int32)
    slot = jnp.arange(tok_dev, dtype=jnp.int32)
    given_key = (perm // group_rows) * tok_dev + slot
    dealt_key = (dealt_position // group_rows) * tok_dev + slot

    def keys(values):
        return values[:, None], values[None, :]

    token_rows = jax.ShapeDtypeStruct((tok_dev, MODEL_WIDTH), bf16)
    move_flops = 2 * tok_dev * tok_dev * MODEL_WIDTH
    gain_row = block_norm_gain[None, :]

    dt_start = 2 * STATE + tensor_rank * heads

    def local_rest(matrix):
        steps = lax.dynamic_slice_in_dim(matrix, dt_start, heads, 1)
        return jnp.concatenate(
            [matrix[:, : 2 * STATE], jnp.pad(steps, ((0, 0), (0, LANES - heads)))], axis=1
        )

    def gather_weight(*shards):
        return lax.all_gather(jnp.concatenate(shards, axis=1), "dp", axis=0, tiled=True)

    w_in = gather_weight(
        gate_input_weight[:, 1, :], gate_input_weight[:, 0, :], local_rest(rest_weight)
    )
    w_out = gather_weight(output_weight.T)
    up_rest = local_rest(adapter_up_rest)
    up_gate = adapter_up_gate_input[:, 0, :]
    up_x = adapter_up_gate_input[:, 1, :]
    taps = jnp.pad(filter_taps_input, ((0, 3), (0, 0)))
    taps_bc = jnp.pad(filter_taps_bc, ((0, 3), (0, 0)))
    head_row = lambda values: jnp.pad(values, (0, LANES - heads))[None, :]
    bias_row, decay_row = head_row(step_bias), head_row(head_decay_rate)
    skip_row = jnp.repeat(skip_weight, HEADDIM)[None, :]
    indicator = jnp.asarray(np.arange(inner)[:, None] // HEADDIM == np.arange(LANES)[None, :], bf16)

    sent_tokens, sent_cotangent = simple_call(
        pack_kernel, (token_rows, token_rows), 2 * move_flops, *keys(dealt_position), tokens, cotangent
    )
    resid, normed_mine = simple_call(
        place_norm_kernel, (token_rows, token_rows), move_flops,
        *keys(given_key), deal(sent_tokens), gain_row,
    )
    normed = gather_rows(normed_mine)
    grad_mine = simple_call(
        unpack_kernel, token_rows, move_flops, *keys(given_key), deal(sent_cotangent)
    )
    grad_full = gather_rows(grad_mine)

    gated_gain = gated_norm_gain[None, :]
    x_act, slope, scan_out, gate_pre, gained, states, bc, dbc, dt, sig, mid_in, square = forward_scan(
        meta, normed, w_in, adapter_down_in, up_x, up_rest, up_gate, taps, taps_bc,
        bias_row, decay_row, skip_row, gated_gain, heads, group_rows, block,
    )
    weighted, gmid, stats = out_grad(
        meta, grad_full, gained, square, w_out, adapter_down_out, adapter_up_out, gated_gain, pairwise
    )
    half_rows = tok_dev if pairwise else group_rows
    gained, _ = lax.optimization_barrier((gained, stats))
    part_sent, part_own = out_project(meta, gained, w_out, adapter_down_out, half_rows)
    stats = sum_tensor(stats)
    if pairwise:
        part_sent, stats = lax.optimization_barrier((part_sent, stats))
        part_other = lax.ppermute(part_sent, "tensor", swap)
    else:
        part_own, part_other = scatter_rows(part_sent)

    gz, grest, gmid_in, gradients = backward_scan(
        meta, scan_out, gate_pre, weighted, x_act, slope, bc, dbc, dt, sig, states, stats,
        normed, mid_in, gained, gmid, taps, taps_bc, decay_row, skip_row, indicator,
        up_gate, up_x, up_rest, heads, inner_all, block,
    )
    part_other, _ = lax.optimization_barrier((part_other, gz))
    sent_output, gup_out = simple_call(
        partial(output_kernel, inner_all=inner_all),
        (token_rows, jax.ShapeDtypeStruct((LANES, MODEL_WIDTH), f32)), 2 * move_flops,
        meta, *keys(perm), resid, part_own, part_other,
        own_rows(stats, 1), grad_mine, adapter_up_out, scalars=1,
    )
    dealt_output = deal(sent_output)
    gradients = lax.dynamic_update_slice(gradients, gup_out, (0, MODEL_WIDTH))
    gz, _ = lax.optimization_barrier((gz, gradients))
    back = partial(project_back, meta, gz, grest, gmid_in, w_in, adapter_down_in, half_rows)
    if pairwise:
        sent_back = back(0)
        grad_other = lax.ppermute(sent_back, "tensor", swap)
        gz, _ = lax.optimization_barrier((gz, sent_back))
        grad_own = project_back(meta, gz, grest, gmid_in, w_in, adapter_down_in, half_rows, 1)
    else:
        grad_own, grad_other = scatter_rows(back(0))
    output = simple_call(unpack_kernel, token_rows, move_flops, *keys(dealt_key), dealt_output)
    grad_other, output = lax.optimization_barrier((grad_other, output))
    sent_grad = simple_call(
        input_grad_kernel, token_rows, move_flops,
        *keys(perm), resid, grad_own, grad_other, grad_mine, gain_row,
    )

    rest_at = 2 * MODEL_WIDTH
    zx_at = rest_at + REST_LOCAL
    out_at = zx_at + 2 * inner
    total = sum_dp(gradients, (sent_back, (grad_own, dealt_output), grad_other) if pairwise else ())
    steps = total[:, rest_at + 2 * STATE : rest_at + 2 * STATE + heads]
    wide = jnp.zeros((total.shape[0], LANES), f32)
    wide = lax.dynamic_update_slice(wide, steps, (0, tensor_rank * heads))
    shared = jnp.concatenate([total[:, : rest_at + 2 * STATE], wide], axis=1)
    share = jnp.concatenate([sum_tensor(shared), total[:, zx_at:]], axis=1)
    share, sent_grad = lax.optimization_barrier((share, sent_grad))
    total = spread_dp(share)
    dealt_grad = deal(sent_grad)
    input_grad, gdown_in, gup_zx, gup_rest, gdown_out, gup_out = simple_call(
        finish_kernel,
        (
            token_rows,
            jax.ShapeDtypeStruct((MODEL_WIDTH, LANES), f32),
            jax.ShapeDtypeStruct((LANES, 2, inner), f32),
            jax.ShapeDtypeStruct((adapter_up_rest.shape[1], LANES), f32),
            jax.ShapeDtypeStruct((inner, LANES), f32),
            jax.ShapeDtypeStruct((LANES, MODEL_WIDTH), f32),
        ),
        move_flops, *keys(dealt_key), dealt_grad, total,
    )
    return output, input_grad, gdown_in, gup_zx, gup_rest.T, gdown_out, gup_out


def solution(mesh):
    placed = (
        P(("dp", "tensor"), None),
        P(("dp", "tensor"), None),
        P(),
        P(),
        P(("dp", "tensor")),
        P(("dp", "tensor")),
        P(),
        P("dp", None, "tensor"),
        P("dp", None),
        P(None, "tensor"),
        P(),
        P("tensor"),
        P("tensor"),
        P("tensor"),
        P("tensor"),
        P("tensor", "dp"),
        P(),
        P(None, None, "tensor"),
        P(),
        P("tensor", None),
        P(),
    )
    return jax.shard_map(
        body,
        mesh=mesh,
        in_specs=placed,
        out_specs=(
            P(("dp", "tensor"), None),
            P(("dp", "tensor"), None),
            P(),
            P(None, None, "tensor"),
            P(),
            P("tensor", None),
            P(),
        ),
        check_vma=False,
    )
```
